128 devices in a mesh: grp: 8 (over z_lo, x), blk: 16 (over z_hi, y, core).
Axes of the slice: x: 4, y: 4, z: 4 (z_hi: 2, z_lo: 2; z = z_hi * 2 + z_lo), core: 2. Of those that a mesh axis runs over, the one named last changes fastest.
Arguments:
- features: float32 [131072, 128], P(('grp', 'blk')), may hold values from -6 to 6
- new_slot: int32 [1024], P(('grp', 'blk')), may hold values from 0 to 1023, as said below
- tile_values: float32 [8, 16, 16, 16, 128, 128], P('grp', 'blk'), may hold values from 0 to 0.04
- tile_dest: int32 [8, 16, 16, 16], P('grp', 'blk'), may hold values from -1 to 63, as said below
- tile_source: int32 [8, 16, 16, 16], P('grp', 'blk'), may hold values from -1 to 7, as said below
- weight: float32 [128, 128], replicated, may hold values from -0.5 to 0.5
- bias_vector: float32 [128], replicated, may hold values from -3 to 3
Outputs:
- activations: float32 [131072, 128], P(('grp', 'blk'))
The draws below stay inside these ranges and needn't reach their ends.
Inputs may be any that keep to these rules, and one draw needn't show every extreme that they name: new_slot is a permutation of the block positions that keeps every block in its range of 128 blocks; the 8 blocks of one device go to at most 16 - 1 devices of its range, at most 1 to any one device, a count that some device reaches; every device's new positions receive exactly 8 blocks. tile_dest[g, b, k, t] is -1 exactly where the slot is empty; the live slots of each (g, b, k) come first, from 1 to 16 of them, and every (g, b) has some k with all 16 live. tile_source is -1 exactly where tile_dest is -1.
All inputs are finite; a program needn't handle non-finite values.
Results may differ from the reference program's by a relative error of at most 0.0003.
Values sent between devices are 32-bit elements; how exact they have to be, the bound alone decides.
No kernel may reach another device: no remote copies, remote signals or barrier semaphores. Data moves between devices by JAX's collectives and lax.ppermute only.
A program may use at most 128 MiB of HBM per device.

```python
import jax
import jax.numpy as jnp
from jax import lax

TILE = 128
FEAT = 128
BLOCKS_DEV = 8
TILE_SLOTS = 16
NODES = 131072
N_GRP = 8
N_BLK = 16


def draw_new_slot(key, part):
    cycle_count = N_BLK
    per_device = BLOCKS_DEV
    runs = cycle_count - 1
    sizes = per_device // runs + (jnp.arange(runs) < per_device % runs).astype(jnp.int32)
    ends = jnp.cumsum(sizes)
    order_ids = jnp.arange(per_device)
    run_of = jnp.sum((ends[None, :] <= order_ids[:, None]).astype(jnp.int32), axis=1)

    def one_group(group_key):
        first_key, second_key, third_key, fourth_key = jax.random.split(group_key, 4)
        offsets = jax.random.permutation(first_key, cycle_count)[:runs]
        rotate = jax.random.permutation(second_key, cycle_count)
        relabel = jax.random.permutation(third_key, cycle_count)
        scores = jax.random.randint(fourth_key, (cycle_count, per_device), 0, 1 << 20) * per_device + order_ids[None, :]
        within = jnp.argsort(scores, axis=1)
        target = relabel[(rotate[:, None] + offsets[run_of][None, :]) % cycle_count]
        landing = within[target, order_ids[None, :]]
        return target * per_device + landing
    tables = jax.vmap(one_group)(jax.random.split(jax.random.fold_in(key, 311), N_GRP))
    base = (jnp.arange(N_GRP) * (N_BLK * BLOCKS_DEV))[:, None, None]
    return (tables + base).reshape(-1).astype(jnp.int32)


def tile_layout(key):
    layout_key = jax.random.fold_in(key, 4242)
    first_key, second_key, third_key, fourth_key = jax.random.split(layout_key, 4)
    shape = (N_GRP, N_BLK, N_BLK)
    counts = jax.random.randint(first_key, shape, 1, TILE_SLOTS + 1)
    full_bucket = jax.random.randint(second_key, (N_GRP, N_BLK), 0, N_BLK)
    counts = jnp.where(jnp.arange(N_BLK)[None, None, :] == full_bucket[:, :, None], TILE_SLOTS, counts)
    live_slots = jnp.arange(TILE_SLOTS)[None, None, None, :] < counts[:, :, :, None]
    targets = jax.random.randint(third_key, shape + (TILE_SLOTS,), 0, N_GRP * BLOCKS_DEV)
    anchors = jax.random.randint(fourth_key, shape + (TILE_SLOTS,), 0, BLOCKS_DEV)
    return (jnp.where(live_slots, targets, -1).astype(jnp.int32), jnp.where(live_slots, anchors, -1).astype(jnp.int32))


def draw_tile_dest(key, part):
    return tile_layout(key)[0]


def draw_tile_source(key, part):
    return tile_layout(key)[1]


def level_of(stream_key, shape, cuts, smallest, high):
    loudness, own = 1.0, jax.random.fold_in(stream_key, 6)
    for dim, shards_of in cuts:
        steps = jnp.exp(jax.random.uniform(jax.random.fold_in(own, dim), (shards_of,), jnp.float32, smallest / len(cuts), high / len(cuts)))
        loudness = loudness * jnp.repeat(steps, shape[dim] // shards_of).reshape([-1 if axis == dim else 1 for axis in range(len(shape))])
    return loudness


def scatter_about(rng, dims, spread, reach, pieces=(), kind=jnp.bfloat16):
    values = spread * jax.random.normal(rng, dims, jnp.float32)
    if pieces:
        values = values * level_of(rng, dims, pieces, -0.22, 0.18)
    return jnp.clip(values, -reach, reach).astype(kind)


def setup_inputs(seed: int = 0) -> dict:
    seeds = jax.random.split(jax.random.key(seed), 8)
    features = scatter_about(seeds[0], (NODES, FEAT), 1.0, 6.0, ((0, 128),), jnp.float32)
    new_slot = draw_new_slot(jax.random.fold_in(seeds[7], 71), 0)
    tile_values = jnp.clip(0.04 * jax.random.uniform(seeds[2], (N_GRP, N_BLK, N_BLK, TILE_SLOTS, TILE, TILE), jnp.float32) ** level_of(seeds[2], (N_GRP, N_BLK, N_BLK, TILE_SLOTS, TILE, TILE), ((0, 8), (1, 16)), -0.2, 0.2), 0.0, 0.04)
    tile_dest = draw_tile_dest(jax.random.fold_in(seeds[7], 71), 0)
    tile_source = draw_tile_source(jax.random.fold_in(seeds[7], 71), 0)
    weight = scatter_about(seeds[5], (FEAT, FEAT), FEAT ** -0.5, 0.5, (), jnp.float32)
    bias_vector = scatter_about(seeds[6], (FEAT,), 0.5, 3.0, (), jnp.float32)
    return dict(features=features, new_slot=new_slot, tile_values=tile_values, tile_dest=tile_dest, tile_source=tile_source, weight=weight, bias_vector=bias_vector)


precise = lax.Precision.HIGHEST


def reference(features, new_slot, tile_values, tile_dest, tile_source, weight, bias_vector):
    range_blocks = N_BLK * BLOCKS_DEV
    all_blocks = N_GRP * range_blocks
    blocks = features.reshape(all_blocks, TILE, FEAT)
    reordered = jnp.zeros_like(blocks).at[new_slot.astype(jnp.int32)].set(blocks)
    devices_all = N_GRP * N_BLK
    device_ids = jnp.arange(devices_all, dtype=jnp.int32)
    group_ids = device_ids // N_BLK
    member_ids = device_ids % N_BLK
    bucket_ids = jnp.arange(N_BLK, dtype=jnp.int32)[:, None]

    def one_device(running, device_item):
        values, targets, anchors, group_id, member_id = device_item
        source_index = (group_id * range_blocks + bucket_ids * BLOCKS_DEV + jnp.maximum(anchors, 0)).astype(jnp.int32)
        clamped = jnp.maximum(targets, 0)
        dest_index = ((clamped // BLOCKS_DEV) * range_blocks + member_id * BLOCKS_DEV + clamped % BLOCKS_DEV).astype(jnp.int32)
        picked = reordered[source_index.reshape(-1)]
        products = jnp.einsum("ntr,nrf->ntf", values.reshape(-1, TILE, TILE).astype(jnp.float32), picked.astype(jnp.float32), precision=precise)
        live_mask = (targets >= 0).astype(jnp.float32).reshape(-1, 1, 1)
        return running.at[dest_index.reshape(-1)].add(products * live_mask), None

    start_sum = jnp.zeros((all_blocks, TILE, FEAT), jnp.float32)
    aggregated, unused = lax.scan(
        one_device,
        start_sum,
        (
            tile_values.reshape(devices_all, N_BLK, TILE_SLOTS, TILE, TILE),
            tile_dest.reshape(devices_all, N_BLK, TILE_SLOTS),
            tile_source.reshape(devices_all, N_BLK, TILE_SLOTS),
            group_ids,
            member_ids,
        ),
    )
    hidden = jnp.dot(aggregated.reshape(-1, FEAT), weight, precision=precise, preferred_element_type=jnp.float32)
    return jax.nn.relu(hidden + bias_vector[None, :])
```

```python
import functools

import jax
import jax.numpy as jnp
from jax import lax
from jax.experimental import pallas as pl
from jax.experimental.pallas import tpu as pltpu
from jax.sharding import Mesh, PartitionSpec as P

TILE = 128
FEAT = 128
BLOCKS = 8
SLOTS = 16
BUCKETS = 16
TILES = BUCKETS * SLOTS
UNROLL = 4
RING = 16
FIRST, SECOND, THIRD = 80, 24, 24
LIST = TILES + UNROLL
DUMMY = 64

AXES = ("z_lo", "x", "z_hi", "y", "core")
AHEAD = [(2 * i + c, 2 * ((i + 1 - 2 * c) % 4) + c) for i in range(4) for c in range(2)]
BACK = [(b, a) for a, b in AHEAD]
SWAP = [(0, 1), (1, 0)]

f32, bf16 = jnp.float32, jnp.bfloat16


def plan_kernel(where, slots, dest, source, lists, counts, table):
    z_lo, x, z_hi, y, core = (where[i] for i in range(5))

    def place(member, carry):
        dz = (member // 8) ^ z_hi
        dc = (member % 2) ^ core
        turn = 1 - 2 * (member % 2)
        dy = ((y - (member // 2) % 4) * turn) & 3
        near = (dy * 2 + dc) * BLOCKS
        side = FIRST - 2 * BLOCKS + dc * BLOCKS
        late = FIRST + dc * SECOND + (dy - 1) * BLOCKS
        base = jnp.where(dz == 0, near, jnp.where(dy == 0, side, late))
        for j in range(BLOCKS):
            table[slots[member * BLOCKS + j] & 127] = base + j
        return carry

    lax.fori_loop(0, BUCKETS, place, 0)

    def bucket(k, carry):
        def one(t, n):
            n0, n1, n2 = n
            at = k * SLOTS + t
            d = dest[at]
            live = d >= 0
            s = table[k * BLOCKS + jnp.maximum(source[at], 0)]
            g = jnp.maximum(d, 0) // BLOCKS
            rel = (((g // 4) ^ z_lo) * 4 + (((g % 4 - x) * (1 - 2 * core)) & 3)) * BLOCKS + (d & 7)
            word = at + s * 256 + rel * 65536
            a, b = s < FIRST, s < FIRST + SECOND
            pos = jnp.where(a, n0, jnp.where(b, LIST + n1, 2 * LIST + n2))
            lists[pos] = word
            inc = live.astype(jnp.int32)
            ia = jnp.where(a, inc, 0)
            ib = jnp.where(a, 0, jnp.where(b, inc, 0))
            return n0 + ia, n1 + ib, n2 + inc - ia - ib

        for t in range(SLOTS):
            carry = one(t, carry)
        return carry

    n = lax.fori_loop(0, BUCKETS, bucket, (0, 0, 0))
    for i in range(3):
        counts[i] = (n[i] + UNROLL - 1) // UNROLL
        for j in range(UNROLL):
            lists[i * LIST + n[i] + j] = (i * FIRST + (SECOND if i == 2 else 0) - (FIRST if i == 2 else 0)) * 256 + DUMMY * 65536


def split(v):
    hi = v.astype(bf16)
    return hi, (v - hi.astype(f32)).astype(bf16)


def product(a, b):
    ah, al = split(a)
    bh, bl = split(b)
    left = jnp.concatenate([ah, al], axis=1)
    right = jnp.concatenate([bh, bl], axis=1)
    both = jnp.dot(left, jnp.concatenate([right, right], axis=0), preferred_element_type=f32)
    return both[:, :FEAT] + both[:, FEAT:]


def tile_kernel(part, base, sizes, n_in, out_sizes, *refs):
    lists, counts, tiles = refs[:3]
    pieces = refs[3 : 3 + len(sizes)]
    refs = refs[3 + len(sizes) :]
    acc_in = refs[0] if n_in else None
    refs = refs[n_in:]
    outs = refs[: len(out_sizes)]
    acc, xs, ring, piece_sem, ring_sem, acc_sem, out_sem = refs[len(out_sizes) :]
    groups = counts[part]

    def fetch(group, slot):
        for j in range(UNROLL):
            at = lists[part * LIST + group * UNROLL + j] & 255
            pltpu.make_async_copy(
                tiles.at[at], ring.at[slot, j], ring_sem.at[slot, j]
            ).start()

    def landed(slot):
        for j in range(UNROLL):
            pltpu.make_async_copy(tiles.at[0], ring.at[slot, j], ring_sem.at[slot, j]).wait()

    depth = RING // UNROLL
    piece_copies = []
    at = 0
    for i, size in enumerate(sizes):
        copy = pltpu.make_async_copy(pieces[i], xs.at[pl.ds(at, size)], piece_sem.at[i])
        copy.start()
        piece_copies.append(copy)
        at += size
    for s in range(depth - 1):
        @pl.when(s < groups)
        def _(s=s):
            fetch(s, s)
    if n_in:
        first = pltpu.make_async_copy(acc_in, acc.at[pl.ds(0, DUMMY)], acc_sem)
        first.start()
    else:
        def clear(d, carry):
            acc[d] = jnp.zeros((TILE, FEAT), f32)
            return carry

        lax.fori_loop(0, DUMMY, clear, 0)
    acc[DUMMY] = jnp.zeros((TILE, FEAT), f32)
    for copy in piece_copies:
        copy.wait()
    if n_in:
        first.wait()

    def step(group, carry):
        slot = group % depth
        ahead = group + depth - 1

        @pl.when(ahead < groups)
        def _():
            fetch(ahead, ahead % depth)

        landed(slot)
        words = [lists[part * LIST + group * UNROLL + j] for j in range(UNROLL)]
        results = [
            product(ring[slot, j], xs[((words[j] >> 8) & 255) - base]) for j in range(UNROLL)
        ]
        for j in range(UNROLL):
            acc[words[j] >> 16] += results[j]
        return carry

    lax.fori_loop(0, groups, step, 0)
    copies = []
    at = 0
    for i, size in enumerate(out_sizes):
        copy = pltpu.make_async_copy(acc.at[pl.ds(at, size)], outs[i], out_sem.at[i])
        copy.start()
        copies.append(copy)
        at += size
    for copy in copies:
        copy.wait()


def tile_products(part, base, lists, counts, tiles, pieces, acc_in, out_sizes):
    sizes = [p.shape[0] for p in pieces]
    n_in = 0 if acc_in is None else 1
    smem = pl.BlockSpec(memory_space=pltpu.SMEM)
    anywhere = pl.BlockSpec(memory_space=pl.ANY)
    return pl.pallas_call(
        functools.partial(tile_kernel, part, base, sizes, n_in, out_sizes),
        out_shape=[jax.ShapeDtypeStruct((n, TILE, FEAT), f32) for n in out_sizes],
        in_specs=[smem, smem] + [anywhere] * (1 + len(sizes) + n_in),
        out_specs=[anywhere] * len(out_sizes),
        scratch_shapes=[
            pltpu.VMEM((DUMMY + 1, TILE, FEAT), f32),
            pltpu.VMEM((sum(sizes), TILE, FEAT), f32),
            pltpu.VMEM((RING // UNROLL, UNROLL, TILE, TILE), f32),
            pltpu.SemaphoreType.DMA((len(sizes),)),
            pltpu.SemaphoreType.DMA((RING // UNROLL, UNROLL)),
            pltpu.SemaphoreType.DMA,
            pltpu.SemaphoreType.DMA((len(out_sizes),)),
        ],
        compiler_params=pltpu.CompilerParams(vmem_limit_bytes=50 * 2**20),
        cost_estimate=pl.CostEstimate(
            flops=2 * TILE * TILE * FEAT * 4 * 60, bytes_accessed=8 * 2**20, transcendentals=0
        ),
    )(lists, counts, tiles, *pieces, *([] if acc_in is None else [acc_in]))


def finish_kernel(a, b, c, d, weight, bias, out):
    total = a[...] + b[...] + c[...] + d[...]
    hidden = product(total.reshape(BLOCKS * TILE, FEAT), weight[...])
    out[...] = jnp.maximum(hidden + bias[...], 0.0)


def after(value, other):
    anywhere = pl.BlockSpec(memory_space=pl.ANY)
    return pl.pallas_call(
        lambda v, o, out: None,
        out_shape=jax.ShapeDtypeStruct(value.shape, value.dtype),
        in_specs=[anywhere, anywhere],
        out_specs=anywhere,
        input_output_aliases={0: 0},
    )(value, other)


def body(features, new_slot, tile_values, tile_dest, tile_source, weight, bias_vector):
    move = lax.ppermute
    where = jnp.stack([lax.axis_index(a) for a in AXES]).astype(jnp.int32)
    own = features.reshape(BLOCKS, TILE, FEAT)
    prim = move(own, ("y", "core"), AHEAD)
    sec = move(own, ("y", "core"), BACK)
    far = move(own, "z_hi", SWAP)
    other = move(own, "core", SWAP)
    wide = new_slot[:, None] + 1024 * lax.broadcasted_iota(jnp.int32, (BLOCKS, 128), 1)
    slots = lax.all_gather(wide, ("z_hi", "y", "core"), axis=0, tiled=True)[:, 0]

    smem = pl.BlockSpec(memory_space=pltpu.SMEM)
    lists, counts = pl.pallas_call(
        plan_kernel,
        out_shape=[
            jax.ShapeDtypeStruct((3 * LIST,), jnp.int32),
            jax.ShapeDtypeStruct((3,), jnp.int32),
        ],
        in_specs=[smem] * 4,
        out_specs=[smem] * 2,
        scratch_shapes=[pltpu.SMEM((128,), jnp.int32)],
    )(where, slots, tile_dest.reshape(TILES), tile_source.reshape(TILES))
    prim = after(prim, lists)

    two = move(prim, ("y", "core"), AHEAD)
    prim_other, sec_other, far_other = [move(p, "core", SWAP) for p in (prim, sec, far)]
    far_prim = move(far, ("y", "core"), AHEAD)
    far_sec = move(far, ("y", "core"), BACK)
    far_two = move(two, "z_hi", SWAP)
    two_other = move(two, "core", SWAP)
    second = [far_prim, far_two, far_sec]
    third = [move(p, "core", SWAP) for p in second]

    tiles = tile_values.reshape(TILES, TILE, TILE)

    first = [own, other, prim, prim_other, two, two_other, sec, sec_other, far, far_other]
    [acc] = tile_products(0, 0, lists, counts, tiles, first, None, [DUMMY])
    [acc] = tile_products(1, FIRST, lists, counts, tiles, second, acc, [DUMMY])
    mine, prim, two, sec, z_mine, z_prim, z_two, z_sec = tile_products(
        2, FIRST + SECOND, lists, counts, tiles, third, acc, [BLOCKS] * 8
    )

    got_two = move(z_two, "z_lo", SWAP)
    got_prim = move(z_prim, ("x", "core"), AHEAD)
    got_sec = move(z_sec, ("x", "core"), BACK)
    got = move(two + got_two, ("x", "core"), AHEAD)
    end_sec = move(sec, ("x", "core"), BACK)
    end_z = move(z_mine + got_prim + got_sec, "z_lo", SWAP)
    end_prim = move(prim + got, ("x", "core"), AHEAD)

    return pl.pallas_call(
        finish_kernel,
        out_shape=jax.ShapeDtypeStruct((BLOCKS * TILE, FEAT), f32),
        compiler_params=pltpu.CompilerParams(vmem_limit_bytes=24 * 2**20),
    )(mine, end_prim, end_sec, end_z, weight, bias_vector.reshape(1, FEAT))


def solution(mesh):
    fine = Mesh(mesh.devices.reshape(2, 4, 2, 4, 2), AXES)
    grp, blk = AXES[:2], AXES[2:]
    return jax.shard_map(
        body,
        mesh=fine,
        in_specs=(
            P(AXES, None),
            P(AXES),
            P(grp, blk, None, None, None, None),
            P(grp, blk, None, None),
            P(grp, blk, None, None),
            P(),
            P(),
        ),
        out_specs=P(AXES, None),
        check_vma=False,
    )
```

```python
import functools

import jax
import jax.numpy as jnp
from jax import lax
from jax.experimental import pallas as pl
from jax.experimental.pallas import tpu as pltpu
from jax.sharding import Mesh, PartitionSpec as P

TILE = 128
FEAT = 128
BLOCKS = 8
SLOTS = 16
BUCKETS = 16
TILES = BUCKETS * SLOTS
UNROLL = 4
RING = 16
FIRST, SECOND, THIRD = 80, 24, 24
LIST = TILES + UNROLL
DUMMY = 64

AXES = ("z_lo", "x", "z_hi", "y", "core")
AHEAD = [(2 * i + c, 2 * ((i + 1 - 2 * c) % 4) + c) for i in range(4) for c in range(2)]
BACK = [(b, a) for a, b in AHEAD]
SWAP = [(0, 1), (1, 0)]

f32, bf16 = jnp.float32, jnp.bfloat16


BASES = (
    (0, 8, 64, 72),
    (16, 56, 80, 120),
    (32, 40, 88, 112),
    (48, 24, 96, 104),
)


def plan_kernel(own, prim, two, sec, packed, lists, counts, table):
    for bases, slots in zip(BASES, (own, prim, two, sec)):
        for i, base in enumerate(bases):
            for j in range(BLOCKS):
                table[slots[i * BLOCKS + j] & 127] = base + j

    def bucket(k, n):
        n0, n1, n2 = n
        for t in range(SLOTS):
            word = packed[k * SLOTS + t]
            inc = (word >= 0).astype(jnp.int32)
            s = table[(word >> 8) & 127]
            a, b = s < FIRST, s < FIRST + SECOND
            lists[jnp.where(a, n0, jnp.where(b, LIST + n1, 2 * LIST + n2))] = (word & 0xFF00FF) | (s << 8)
            ia = jnp.where(a, inc, 0)
            ib = jnp.where(b, inc, 0)
            n0, n1, n2 = n0 + ia, n1 + ib - ia, n2 + inc - ib
        return n0, n1, n2

    n = lax.fori_loop(0, BUCKETS, bucket, (0, 0, 0))
    for i, base in enumerate((0, FIRST, FIRST + SECOND)):
        counts[i] = (n[i] + UNROLL - 1) // UNROLL
        for j in range(UNROLL):
            lists[i * LIST + n[i] + j] = base * 256 + DUMMY * 65536


def split(v):
    hi = v.astype(bf16)
    return hi, (v - hi.astype(f32)).astype(bf16)


def halves(v):
    return jnp.concatenate(split(v), axis=1)


def product(a, right):
    both = jnp.dot(halves(a), jnp.concatenate([right, right], axis=0), preferred_element_type=f32)
    return both[:, :FEAT] + both[:, FEAT:]


def tile_kernel(part, base, n_pieces, n_in, n_parts, *refs):
    lists, counts, tiles = refs[:3]
    pieces = refs[3 : 3 + n_pieces]
    *parts, acc, xs, ring, ring_sem = refs[3 + n_pieces + n_in :]
    groups = counts[part]
    depth = RING // UNROLL

    def fetch(group, slot):
        for j in range(UNROLL):
            at = lists[part * LIST + group * UNROLL + j] & 255
            pltpu.make_async_copy(tiles.at[at], ring.at[slot, j], ring_sem.at[slot, j]).start()

    def landed(slot):
        for j in range(UNROLL):
            pltpu.make_async_copy(tiles.at[0], ring.at[slot, j], ring_sem.at[slot, j]).wait()

    for s in range(depth - 1):

        @pl.when(s < groups)
        def _(s=s):
            fetch(s, s)

    def halve(j, carry):
        for i, piece in enumerate(pieces):
            xs[i * BLOCKS + j] = halves(piece[j])
        return carry

    lax.fori_loop(0, BLOCKS, halve, 0)

    def begin(d, carry):
        acc[d] = refs[3 + n_pieces][d] if n_in else jnp.zeros((TILE, FEAT), f32)
        return carry

    lax.fori_loop(0, DUMMY + 1, begin, 0, unroll=5)

    def step(group, carry):
        slot = group % depth
        ahead = group + depth - 1

        @pl.when(ahead < groups)
        def _():
            fetch(ahead, ahead % depth)

        landed(slot)
        words = [lists[part * LIST + group * UNROLL + j] for j in range(UNROLL)]
        results = [
            product(ring[slot, j], xs[((words[j] >> 8) & 255) - base]) for j in range(UNROLL)
        ]
        for j in range(UNROLL):
            acc[words[j] >> 16] += results[j]
        return carry

    lax.fori_loop(0, groups, step, 0)
    if n_parts:

        def hand_out(j, carry):
            for i, out in enumerate(parts):
                out[j] = acc[i * BLOCKS + j]
            return carry

        lax.fori_loop(0, BLOCKS, hand_out, 0)


def tile_products(part, base, lists, counts, tiles, pieces, acc_in, n_parts):
    n_in = 0 if acc_in is None else 1
    smem = pl.BlockSpec(memory_space=pltpu.SMEM)
    vmem = pl.BlockSpec(memory_space=pltpu.VMEM)
    hbm = pl.BlockSpec(memory_space=pltpu.HBM)
    return pl.pallas_call(
        functools.partial(tile_kernel, part, base, len(pieces), n_in, n_parts),
        out_shape=[jax.ShapeDtypeStruct((BLOCKS, TILE, FEAT), f32)] * n_parts
        or [jax.ShapeDtypeStruct((DUMMY + 1, TILE, FEAT), f32)],
        in_specs=[smem, smem, hbm] + [vmem] * (len(pieces) + n_in),
        out_specs=[vmem] * max(1, n_parts),
        scratch_shapes=[pltpu.VMEM((DUMMY + 1, TILE, FEAT), f32)] * (n_parts > 0)
        + [
            pltpu.VMEM((len(pieces) * BLOCKS, TILE, 2 * FEAT), bf16),
            pltpu.VMEM((RING // UNROLL, UNROLL, TILE, TILE), f32),
            pltpu.SemaphoreType.DMA((RING // UNROLL, UNROLL)),
        ],
        compiler_params=pltpu.CompilerParams(vmem_limit_bytes=40 * 2**20),
        cost_estimate=pl.CostEstimate(
            flops=2 * TILE * TILE * FEAT * 4 * 60, bytes_accessed=8 * 2**20, transcendentals=0
        ),
    )(lists, counts, tiles, *pieces, *([] if acc_in is None else [acc_in]))


def finish_kernel(a, b, c, d, weight, bias, out):
    total = a[...] + b[...] + c[...] + d[...]
    hidden = product(total.reshape(BLOCKS * TILE, FEAT), halves(weight[...]))
    out[...] = jnp.maximum(hidden + bias[...], 0.0)


def after(value, *others):
    return lax.optimization_barrier((value, *others))[0]


def body(features, new_slot, tile_values, tile_dest, tile_source, weight, bias_vector):
    move = lax.ppermute
    own = features.reshape(BLOCKS, TILE, FEAT)
    prim = move(own, ("y", "core"), AHEAD)
    sec = move(own, ("y", "core"), BACK)
    far = move(own, "z_hi", SWAP)
    other = move(own, "core", SWAP)

    slots = jnp.concatenate([new_slot, move(new_slot, "core", SWAP)])
    slots = jnp.concatenate([slots, move(slots, "z_hi", SWAP)])
    slots_prim = move(slots, ("y", "core"), AHEAD)
    slots_sec = move(slots, ("y", "core"), BACK)
    slots_two = move(slots_prim, ("y", "core"), AHEAD)

    z_lo, x, core = (lax.axis_index(a) for a in ("z_lo", "x", "core"))
    bucket = lax.broadcasted_iota(jnp.int32, (BUCKETS, SLOTS), 0)
    slot = lax.broadcasted_iota(jnp.int32, (BUCKETS, SLOTS), 1)
    dest = tile_dest.reshape(BUCKETS, SLOTS)
    group = dest >> 3
    turned = (((group >> 2) ^ z_lo) * 4 + (((group & 3) - x) * (1 - 2 * core) & 3)) * BLOCKS + (dest & 7)
    position = bucket * BLOCKS + tile_source.reshape(BUCKETS, SLOTS)
    packed = jnp.where(dest >= 0, (bucket * SLOTS + slot) + position * 256 + turned * 65536, -1)

    smem = pl.BlockSpec(memory_space=pltpu.SMEM)
    lists, counts = pl.pallas_call(
        plan_kernel,
        out_shape=[
            jax.ShapeDtypeStruct((3 * LIST,), jnp.int32),
            jax.ShapeDtypeStruct((3,), jnp.int32),
        ],
        in_specs=[smem] * 5,
        out_specs=[smem] * 2,
        scratch_shapes=[pltpu.SMEM((128,), jnp.int32)],
        cost_estimate=pl.CostEstimate(flops=10**7, bytes_accessed=10**4, transcendentals=0),
    )(slots, slots_prim, slots_two, slots_sec, packed.reshape(TILES))

    prim = after(prim, slots_two)
    two = move(prim, ("y", "core"), AHEAD)
    prim_other, sec_other, far_other = [move(p, "core", SWAP) for p in (prim, sec, far)]
    far = after(far, two, lists)
    far_prim = move(far, ("y", "core"), AHEAD)
    far_sec = move(far, ("y", "core"), BACK)
    far_two = move(two, "z_hi", SWAP)
    two_other = move(two, "core", SWAP)
    second = [far_prim, far_two, far_sec]
    third = [move(p, "core", SWAP) for p in second]

    tiles = tile_values.reshape(TILES, TILE, TILE)
    first = [own, other, prim, prim_other, two, two_other, sec, sec_other, far, far_other]
    [acc] = tile_products(0, 0, lists, counts, tiles, first, None, 0)
    [acc] = tile_products(1, FIRST, lists, counts, tiles, second, acc, 0)
    mine, prim, two, sec, z_mine, z_prim, z_two, z_sec = tile_products(
        2, FIRST + SECOND, lists, counts, tiles, third, acc, 8
    )

    got_two = move(z_two, "z_lo", SWAP)
    got_prim = move(z_prim, ("x", "core"), AHEAD)
    got_sec = move(z_sec, ("x", "core"), BACK)
    got = move(two + got_two, ("x", "core"), AHEAD)
    end_sec = move(sec, ("x", "core"), BACK)
    end_z = move(z_mine + got_prim + got_sec, "z_lo", SWAP)
    end_prim = move(prim + got, ("x", "core"), AHEAD)

    return pl.pallas_call(
        finish_kernel,
        out_shape=jax.ShapeDtypeStruct((BLOCKS * TILE, FEAT), f32),
        compiler_params=pltpu.CompilerParams(vmem_limit_bytes=24 * 2**20),
    )(mine, end_prim, end_sec, end_z, weight, bias_vector.reshape(1, FEAT))


def solution(mesh):
    fine = Mesh(mesh.devices.reshape(2, 4, 2, 4, 2), AXES)
    grp, blk = AXES[:2], AXES[2:]
    return jax.shard_map(
        body,
        mesh=fine,
        in_specs=(
            P(AXES, None),
            P(AXES),
            P(grp, blk, None, None, None, None),
            P(grp, blk, None, None),
            P(grp, blk, None, None),
            P(),
            P(),
        ),
        out_specs=P(AXES, None),
        check_vma=False,
    )
```

```python
import functools

import jax
import jax.numpy as jnp
from jax import lax
from jax.experimental import pallas as pl
from jax.experimental.pallas import tpu as pltpu
from jax.sharding import Mesh, PartitionSpec as P

TILE = 128
FEAT = 128
BLOCKS = 8
SLOTS = 16
BUCKETS = 16
TILES = BUCKETS * SLOTS
UNROLL = 4
RING = 16
DUMMY = 64

AXES = ("z_lo", "x", "z_hi", "y", "core")
AHEAD = [(2 * i + c, 2 * ((i + 1 - 2 * c) % 4) + c) for i in range(4) for c in range(2)]
BACK = [(b, a) for a, b in AHEAD]
SWAP = [(0, 1), (1, 0)]

f32, bf16 = jnp.float32, jnp.bfloat16


def live_kernel(packed, words, count):
    def bucket(k, n):
        for t in range(SLOTS):
            word = packed[k * SLOTS + t]
            words[n] = word
            n = n + (word >= 0).astype(jnp.int32)
        return n

    count[0] = lax.fori_loop(0, BUCKETS, bucket, 0)


def split(v):
    hi = v.astype(bf16)
    return hi, (v - hi.astype(f32)).astype(bf16)


def halves(v):
    return jnp.concatenate(split(v), axis=1)


def product(a, right):
    both = jnp.dot(halves(a), jnp.concatenate([right, right], axis=0), preferred_element_type=f32)
    return both[:, :FEAT] + both[:, FEAT:]


def tile_kernel(n_pieces, first, last, *refs):
    words, count, tiles = refs[:3]
    pieces = refs[3 : 3 + n_pieces]
    so_far = None if first else refs[3 + n_pieces]
    outs = refs[4 + n_pieces - first :]
    if last:
        parts, (acc, rest, left) = outs[:BLOCKS], outs[BLOCKS : BLOCKS + 3]
        scratch = outs[BLOCKS + 3 :]
    else:
        acc, rest, left = outs[:3]
        scratch = outs[3:]
    xs, ring, slots, table, mine, ring_sem, slot_sem = scratch
    depth = RING // UNROLL

    reads = [
        pltpu.make_async_copy(piece.at[pl.ds(BLOCKS * TILE, 8)], slots.at[i], slot_sem.at[i])
        for i, piece in enumerate(pieces)
    ]
    for read in reads:
        read.start()
    for p in range(BUCKETS * BLOCKS):
        table[p] = -1
    for read in reads:
        read.wait()
    for i in range(n_pieces):
        for j in range(BLOCKS):
            table[slots[i, 0, j].astype(jnp.int32) & 127] = i * BLOCKS + j

    def sort(at, n):
        here, there = n
        word = words[at]
        s = table[(word >> 8) & 127]
        known = (s >= 0).astype(jnp.int32)
        mine[here] = (word & 0xFF00FF) | (s << 8)
        rest[there] = word
        return here + known, there + 1 - known

    def sort4(group, n):
        for j in range(4):
            n = sort(group * 4 + j, n)
        return n

    total = count[0]
    n = lax.fori_loop(0, total // 4, sort4, (0, 0))
    here, there = lax.fori_loop(total // 4 * 4, total, sort, n)
    left[0] = there
    for j in range(UNROLL):
        mine[here + j] = DUMMY * 65536
    groups = (here + UNROLL - 1) // UNROLL

    def fetch(group, slot):
        for j in range(UNROLL):
            at = mine[group * UNROLL + j] & 255
            pltpu.make_async_copy(tiles.at[at], ring.at[slot, j], ring_sem.at[slot, j]).start()

    def landed(slot):
        for j in range(UNROLL):
            pltpu.make_async_copy(tiles.at[0], ring.at[slot, j], ring_sem.at[slot, j]).wait()

    for s in range(depth - 1):

        @pl.when(s < groups)
        def _(s=s):
            fetch(s, s)

    def halve(j, carry):
        for i, piece in enumerate(pieces):
            xs[i * BLOCKS + j] = halves(piece[pl.ds(pl.multiple_of(j * TILE, TILE), TILE), :])
        return carry

    lax.fori_loop(0, BLOCKS, halve, 0)

    def begin(d, carry):
        acc[d] = jnp.zeros((TILE, FEAT), f32) if first else so_far[d]
        return carry

    lax.fori_loop(0, DUMMY + 1, begin, 0, unroll=5)

    def step(group, carry):
        slot = group % depth
        ahead = group + depth - 1

        @pl.when(ahead < groups)
        def _():
            fetch(ahead, ahead % depth)

        landed(slot)
        own = [mine[group * UNROLL + j] for j in range(UNROLL)]
        results = [product(ring[slot, j], xs[(own[j] >> 8) & 127]) for j in range(UNROLL)]
        for j in range(UNROLL):
            acc[own[j] >> 16] += results[j]
        return carry

    lax.fori_loop(0, groups, step, 0)
    if last:

        def hand_out(j, carry):
            for i, out in enumerate(parts):
                out[j] = acc[i * BLOCKS + j]
            return carry

        lax.fori_loop(0, BLOCKS, hand_out, 0)


def tile_products(words, count, tiles, pieces, so_far=None, last=False):
    first = so_far is None
    smem = pl.BlockSpec(memory_space=pltpu.SMEM)
    vmem = pl.BlockSpec(memory_space=pltpu.VMEM)
    hbm = pl.BlockSpec(memory_space=pltpu.HBM)
    sums = pltpu.VMEM((DUMMY + 1, TILE, FEAT), f32)
    going_on = [pltpu.SMEM((TILES + 8,), jnp.int32), pltpu.SMEM((1,), jnp.int32)]
    part = jax.ShapeDtypeStruct((BLOCKS, TILE, FEAT), f32)
    return pl.pallas_call(
        functools.partial(tile_kernel, len(pieces), first, last),
        out_shape=[part] * BLOCKS
        if last
        else [jax.ShapeDtypeStruct(r.shape, r.dtype) for r in (sums, *going_on)],
        in_specs=[smem, smem, hbm] + [vmem] * (len(pieces) + (not first)),
        out_specs=[vmem] * BLOCKS if last else [vmem, smem, smem],
        scratch_shapes=([sums, *going_on] if last else [])
        + [
            pltpu.VMEM((len(pieces) * BLOCKS, TILE, 2 * FEAT), bf16),
            pltpu.VMEM((RING // UNROLL, UNROLL, TILE, TILE), f32),
            pltpu.SMEM((len(pieces), 8, 128), f32),
            pltpu.SMEM((BUCKETS * BLOCKS,), jnp.int32),
            pltpu.SMEM((TILES + 8,), jnp.int32),
            pltpu.SemaphoreType.DMA((RING // UNROLL, UNROLL)),
            pltpu.SemaphoreType.DMA((len(pieces),)),
        ],
        compiler_params=pltpu.CompilerParams(vmem_limit_bytes=40 * 2**20),
        cost_estimate=pl.CostEstimate(
            flops=2 * TILE * TILE * FEAT * 4 * 60, bytes_accessed=8 * 2**20, transcendentals=0
        ),
    )(words, count, tiles, *pieces, *([] if first else [so_far]))


def finish_kernel(a, b, c, d, weight, bias, out):
    total = a[...] + b[...] + c[...] + d[...]
    hidden = product(total.reshape(BLOCKS * TILE, FEAT), halves(weight[...]))
    out[...] = jnp.maximum(hidden + bias[...], 0.0)


def after(value, *others):
    return lax.optimization_barrier((value, *others))[0]


def body(features, new_slot, tile_values, tile_dest, tile_source, weight, bias_vector):
    move = lax.ppermute
    row = jnp.pad(new_slot.astype(f32)[None, :], ((0, 7), (0, FEAT - BLOCKS)))
    own = jnp.concatenate([features, row])
    prim = move(own, ("y", "core"), AHEAD)
    sec = move(own, ("y", "core"), BACK)
    far = move(own, "z_hi", SWAP)
    other = move(own, "core", SWAP)

    z_lo, x, core = (lax.axis_index(a) for a in ("z_lo", "x", "core"))
    bucket = lax.broadcasted_iota(jnp.int32, (BUCKETS, SLOTS), 0)
    slot = lax.broadcasted_iota(jnp.int32, (BUCKETS, SLOTS), 1)
    dest = tile_dest.reshape(BUCKETS, SLOTS)
    group = dest >> 3
    turned = (((group >> 2) ^ z_lo) * 4 + (((group & 3) - x) * (1 - 2 * core) & 3)) * BLOCKS + (dest & 7)
    position = bucket * BLOCKS + tile_source.reshape(BUCKETS, SLOTS)
    packed = jnp.where(dest >= 0, (bucket * SLOTS + slot) + position * 256 + turned * 65536, -1)

    smem = pl.BlockSpec(memory_space=pltpu.SMEM)
    words, count = pl.pallas_call(
        live_kernel,
        out_shape=[
            jax.ShapeDtypeStruct((TILES + 8,), jnp.int32),
            jax.ShapeDtypeStruct((1,), jnp.int32),
        ],
        in_specs=[smem],
        out_specs=[smem] * 2,
        cost_estimate=pl.CostEstimate(flops=10**7, bytes_accessed=10**4, transcendentals=0),
    )(packed.reshape(TILES))

    prim = after(prim, words)
    two = move(prim, ("y", "core"), AHEAD)
    prim_other, sec_other, far_other = [move(p, "core", SWAP) for p in (prim, sec, far)]
    far_now = after(far, two)
    far_prim = move(far_now, ("y", "core"), AHEAD)
    far_sec = move(far_now, ("y", "core"), BACK)
    far_two = move(two, "z_hi", SWAP)
    two_other = move(two, "core", SWAP)

    tiles = tile_values.reshape(TILES, TILE, TILE)
    near = [own, other, prim, prim_other, two, two_other, sec, sec_other, far, far_other]
    sums, words, count = tile_products(words, count, tiles, near)
    second = [after(p, sums) for p in (far_prim, far_sec, far_two)]
    third = [move(p, "core", SWAP) for p in second]
    sums, words, count = tile_products(words, count, tiles, second, sums)
    mine, prim, two, sec, z_mine, z_prim, z_two, z_sec = tile_products(
        words, count, tiles, third, sums, last=True
    )

    got_two = move(z_two, "z_lo", SWAP)
    got_prim = move(z_prim, ("x", "core"), AHEAD)
    got_sec = move(z_sec, ("x", "core"), BACK)
    got = move(two + got_two, ("x", "core"), AHEAD)
    end_sec = move(after(sec, got), ("x", "core"), BACK)
    end_z = move(z_mine + got_prim + got_sec, "z_lo", SWAP)
    end_prim = move(prim + got, ("x", "core"), AHEAD)

    return pl.pallas_call(
        finish_kernel,
        out_shape=jax.ShapeDtypeStruct((BLOCKS * TILE, FEAT), f32),
        compiler_params=pltpu.CompilerParams(vmem_limit_bytes=24 * 2**20),
    )(mine, end_prim, end_sec, end_z, weight, bias_vector.reshape(1, FEAT))


def solution(mesh):
    fine = Mesh(mesh.devices.reshape(2, 4, 2, 4, 2), AXES)
    grp, blk = AXES[:2], AXES[2:]
    return jax.shard_map(
        body,
        mesh=fine,
        in_specs=(
            P(AXES, None),
            P(AXES),
            P(grp, blk, None, None, None, None),
            P(grp, blk, None, None),
            P(grp, blk, None, None),
            P(),
            P(),
        ),
        out_specs=P(AXES, None),
        check_vma=False,
    )
```

```python
import functools

import jax
import jax.numpy as jnp
from jax import lax
from jax.experimental import pallas as pl
from jax.experimental.pallas import tpu as pltpu
from jax.sharding import Mesh, PartitionSpec as P

TILE = 128
FEAT = 128
BLOCKS = 8
SLOTS = 16
BUCKETS = 16
TILES = BUCKETS * SLOTS
UNROLL = 8
AHEAD_BY = 8
GROUP = 4
DUMMY = 64

AXES = ("z_lo", "x", "z_hi", "y", "core")
UP = [(i, (i + 1) % 4) for i in range(4)]
DOWN = [(i, (i - 1) % 4) for i in range(4)]
SWAP = [(0, 1), (1, 0)]

f32, bf16 = jnp.float32, jnp.bfloat16


def split(v):
    hi = v.astype(bf16)
    return hi, (v - hi.astype(f32)).astype(bf16)


def halves(v):
    return jnp.concatenate(split(v), axis=1)


def product(left, right):
    both = jnp.dot(left, jnp.concatenate([right, right], axis=0), preferred_element_type=f32)
    return both[:, :FEAT] + both[:, FEAT:]


def live_kernel(packed, tiles, words, count, split_tiles, at, ring, sem):
    def bucket(k, n):
        loaded = [packed[k * SLOTS + t] for t in range(SLOTS)]
        for t, word in enumerate(loaded):
            at[n] = word & 255
            words[n] = (word & 0xFFFF00) | n
            n = n + (word >= 0).astype(jnp.int32)
        return n

    total = lax.fori_loop(0, BUCKETS, bucket, 0)
    count[0] = total
    for j in range(UNROLL):
        words[total + j] = -1
        at[total + j] = 0
    groups = (total + GROUP - 1) // GROUP

    def fetch(group, slot):
        for j in range(GROUP):
            pltpu.make_async_copy(tiles.at[at[group * GROUP + j]], ring.at[slot, j], sem.at[slot, j]).start()

    for s in range(AHEAD_BY - 1):

        @pl.when(s < groups)
        def _(s=s):
            fetch(s, s)

    def step(group, carry):
        slot = group % AHEAD_BY
        ahead = group + AHEAD_BY - 1

        @pl.when(ahead < groups)
        def _():
            fetch(ahead, ahead % AHEAD_BY)

        for j in range(GROUP):
            pltpu.make_async_copy(tiles.at[0], ring.at[slot, j], sem.at[slot, j]).wait()
        for j in range(GROUP):
            split_tiles[group * GROUP + j] = halves(ring[slot, j])
        return carry

    lax.fori_loop(0, groups, step, 0)


def tile_kernel(n_pieces, first, last, *refs):
    words, count, tiles = refs[:3]
    pieces = refs[3 : 3 + n_pieces]
    so_far = None if first else refs[3 + n_pieces]
    outs = refs[4 + n_pieces - first :]
    if last:
        parts, (acc, rest, left) = outs[:BLOCKS], outs[BLOCKS : BLOCKS + 3]
        scratch = outs[BLOCKS + 3 :]
    else:
        acc, rest, left = outs[:3]
        scratch = outs[3:]
    xs, slots, table, mine, slot_sem = scratch

    reads = [
        pltpu.make_async_copy(piece.at[pl.ds(BLOCKS * TILE, 8)], slots.at[i], slot_sem.at[i])
        for i, piece in enumerate(pieces)
    ]
    for read in reads:
        read.start()
    for p in range(BUCKETS * BLOCKS):
        table[p] = -1
    for read in reads:
        read.wait()
    for i in range(n_pieces):
        for j in range(BLOCKS):
            table[slots[i, 0, j].astype(jnp.int32) & 127] = i * BLOCKS + j

    def sort(group, n):
        here, there = n
        loaded = [words[group * UNROLL + j] for j in range(UNROLL)]
        found = [table[(word >> 8) & 127] for word in loaded]
        for word, s in zip(loaded, found):
            live = (word >= 0).astype(jnp.int32)
            known = jnp.where(s >= 0, live, 0)
            mine[here] = (word & 0xFF00FF) | (s << 8)
            rest[there] = word
            here, there = here + known, there + live - known
        return here, there

    here, there = lax.fori_loop(0, (count[0] + UNROLL - 1) // UNROLL, sort, (0, 0))
    left[0] = there
    for j in range(UNROLL):
        mine[here + j] = DUMMY * 65536
        rest[there + j] = -1

    def halve(j, carry):
        for i, piece in enumerate(pieces):
            xs[i * BLOCKS + j] = halves(piece[pl.ds(pl.multiple_of(j * TILE, TILE), TILE), :])
        return carry

    lax.fori_loop(0, BLOCKS, halve, 0)

    def begin(d, carry):
        acc[d] = jnp.zeros((TILE, FEAT), f32) if first else so_far[d]
        return carry

    lax.fori_loop(0, DUMMY + 1, begin, 0, unroll=5)

    def step(group, carry):
        own = [mine[group * UNROLL + j] for j in range(UNROLL)]
        results = [product(tiles[w & 255], xs[(w >> 8) & 127]) for w in own]
        for w, result in zip(own, results):
            acc[w >> 16] += result
        return carry

    lax.fori_loop(0, (here + UNROLL - 1) // UNROLL, step, 0)
    if last:

        def hand_out(j, carry):
            for i, out in enumerate(parts):
                out[j] = acc[i * BLOCKS + j]
            return carry

        lax.fori_loop(0, BLOCKS, hand_out, 0)


def tile_products(words, count, tiles, pieces, so_far=None, last=False):
    first = so_far is None
    smem = pl.BlockSpec(memory_space=pltpu.SMEM)
    vmem = pl.BlockSpec(memory_space=pltpu.VMEM)
    sums = pltpu.VMEM((DUMMY + 1, TILE, FEAT), f32)
    going_on = [pltpu.SMEM((TILES + 2 * UNROLL,), jnp.int32), pltpu.SMEM((1,), jnp.int32)]
    part = jax.ShapeDtypeStruct((BLOCKS, TILE, FEAT), f32)
    return pl.pallas_call(
        functools.partial(tile_kernel, len(pieces), first, last),
        out_shape=[part] * BLOCKS
        if last
        else [jax.ShapeDtypeStruct(r.shape, r.dtype) for r in (sums, *going_on)],
        in_specs=[smem, smem] + [vmem] * (1 + len(pieces) + (not first)),
        out_specs=[vmem] * BLOCKS if last else [vmem, smem, smem],
        scratch_shapes=([sums, *going_on] if last else [])
        + [
            pltpu.VMEM((len(pieces) * BLOCKS, TILE, 2 * FEAT), bf16),
            pltpu.SMEM((len(pieces), 8, 128), f32),
            pltpu.SMEM((BUCKETS * BLOCKS,), jnp.int32),
            pltpu.SMEM((TILES + 2 * UNROLL,), jnp.int32),
            pltpu.SemaphoreType.DMA((len(pieces),)),
        ],
        compiler_params=pltpu.CompilerParams(vmem_limit_bytes=16 * 2**20),
        cost_estimate=pl.CostEstimate(
            flops=2 * TILE * TILE * FEAT * 4 * 60, bytes_accessed=8 * 2**20, transcendentals=0
        ),
    )(words, count, tiles, *pieces, *([] if first else [so_far]))


def finish_kernel(a, b, c, d, weight, bias, out):
    total = a[...] + b[...] + c[...] + d[...]
    hidden = product(halves(total.reshape(BLOCKS * TILE, FEAT)), halves(weight[...]))
    out[...] = jnp.maximum(hidden + bias[...], 0.0)


def after(value, *others):
    return lax.optimization_barrier((value, *others))[0]


def body(features, new_slot, tile_values, tile_dest, tile_source, weight, bias_vector):
    move = lax.ppermute
    row = jnp.pad(new_slot.astype(f32)[None, :], ((0, 7), (0, FEAT - BLOCKS)))
    own = jnp.concatenate([features, row])
    below = move(own, "y", UP)
    above = move(own, "y", DOWN)
    far = move(own, "z_hi", SWAP)
    other = move(own, "core", SWAP)

    z_lo, x = lax.axis_index("z_lo"), lax.axis_index("x")
    bucket = lax.broadcasted_iota(jnp.int32, (BUCKETS, SLOTS), 0)
    slot = lax.broadcasted_iota(jnp.int32, (BUCKETS, SLOTS), 1)
    dest = tile_dest.reshape(BUCKETS, SLOTS)
    group = dest >> 3
    turned = (((group >> 2) ^ z_lo) * 4 + ((group & 3) - x & 3)) * BLOCKS + (dest & 7)
    position = bucket * BLOCKS + tile_source.reshape(BUCKETS, SLOTS)
    packed = jnp.where(dest >= 0, (bucket * SLOTS + slot) + position * 256 + turned * 65536, -1)

    smem = pl.BlockSpec(memory_space=pltpu.SMEM)
    words, count, tiles = pl.pallas_call(
        live_kernel,
        out_shape=[
            jax.ShapeDtypeStruct((TILES + 2 * UNROLL,), jnp.int32),
            jax.ShapeDtypeStruct((1,), jnp.int32),
            jax.ShapeDtypeStruct((TILES + GROUP, TILE, 2 * TILE), bf16),
        ],
        in_specs=[smem, pl.BlockSpec(memory_space=pltpu.HBM)],
        out_specs=[smem, smem, pl.BlockSpec(memory_space=pltpu.VMEM)],
        scratch_shapes=[
            pltpu.SMEM((TILES + 2 * UNROLL,), jnp.int32),
            pltpu.VMEM((AHEAD_BY, GROUP, TILE, TILE), f32),
            pltpu.SemaphoreType.DMA((AHEAD_BY, GROUP)),
        ],
        compiler_params=pltpu.CompilerParams(vmem_limit_bytes=20 * 2**20),
        cost_estimate=pl.CostEstimate(flops=10**7, bytes_accessed=16 * 2**20, transcendentals=0),
    )(packed.reshape(TILES), tile_values.reshape(TILES, TILE, TILE))

    below = after(below, words)
    two = move(below, "y", UP)
    far_above = move(far, "y", DOWN)
    far_below = move(below, "z_hi", SWAP)
    swapped = [move(p, "core", SWAP) for p in (below, above, far)]
    sums, words, count = tile_products(words, count, tiles, [own, other, below, above, far, *swapped])

    two = after(two, sums)
    far_two = move(two, "z_hi", SWAP)
    late = [two, far_above, far_below]
    swapped = [move(p, "core", SWAP) for p in late]
    sums, words, count = tile_products(words, count, tiles, [*late, *swapped], sums)

    far_two = after(far_two, sums)
    mine, up, two, down, z_mine, z_up, z_two, z_down = tile_products(
        words, count, tiles, [far_two, move(far_two, "core", SWAP)], sums, last=True
    )

    got_two = move(z_two, "z_lo", SWAP)
    got_down = move(z_down, "x", DOWN)
    end_down = move(down, "x", DOWN)
    got_up = move(after(z_up, got_two), "z_lo", SWAP)
    got = move(two + got_two, "x", UP)
    end_z = move(z_mine + got_down, "z_lo", SWAP)
    end_up = move(up + got + got_up, "x", UP)

    return pl.pallas_call(
        finish_kernel,
        out_shape=jax.ShapeDtypeStruct((BLOCKS * TILE, FEAT), f32),
        compiler_params=pltpu.CompilerParams(vmem_limit_bytes=24 * 2**20),
    )(mine, end_up, end_down, end_z, weight, bias_vector.reshape(1, FEAT))


def solution(mesh):
    fine = Mesh(mesh.devices.reshape(2, 4, 2, 4, 2), AXES)
    grp, blk = AXES[:2], AXES[2:]
    return jax.shard_map(
        body,
        mesh=fine,
        in_specs=(
            P(AXES, None),
            P(AXES),
            P(grp, blk, None, None, None, None),
            P(grp, blk, None, None),
            P(grp, blk, None, None),
            P(),
            P(),
        ),
        out_specs=P(AXES, None),
        check_vma=False,
    )
```

```python
import functools

import jax
import jax.numpy as jnp
from jax import lax
from jax.experimental import pallas as pl
from jax.experimental.pallas import tpu as pltpu
from jax.sharding import Mesh, PartitionSpec as P

TILE = 128
FEAT = 128
BLOCKS = 8
SLOTS = 16
BUCKETS = 16
TILES = BUCKETS * SLOTS
UNROLL = 8
DEPTH = 6
DUMMY = 64

AXES = ("z_lo", "x", "z_hi", "y", "core")
UP = [(i, (i + 1) % 4) for i in range(4)]
DOWN = [(i, (i - 1) % 4) for i in range(4)]
SWAP = [(0, 1), (1, 0)]

f32, bf16 = jnp.float32, jnp.bfloat16


def split(v):
    hi = v.astype(bf16)
    return hi, (v - hi.astype(f32)).astype(bf16)


def halves(v):
    return jnp.concatenate(split(v), axis=1)


def product(left, right):
    both = jnp.dot(left, jnp.concatenate([right, right], axis=0), preferred_element_type=f32)
    return both[:, :FEAT] + both[:, FEAT:]


def live_kernel(dest, source, words, count):
    def bucket(k, n):
        loaded = [(dest[k, t], source[k, t]) for t in range(SLOTS)]
        for t, (d, s) in enumerate(loaded):
            words[n] = (k * SLOTS + t) + (k * BLOCKS + s) * 256 + d * 65536
            n = n + (d >= 0).astype(jnp.int32)
        return n

    total = lax.fori_loop(0, BUCKETS, bucket, 0)
    count[0] = total
    for j in range(UNROLL):
        words[total + j] = -1


def tile_kernel(n_pieces, first, last, *refs):
    place, words, count, tiles = refs[:4]
    refs = refs[1:]
    pieces = refs[3 : 3 + n_pieces]
    so_far = None if first else refs[3 + n_pieces]
    outs = refs[4 + n_pieces - first :]
    if last:
        parts, (acc, rest, left) = outs[:BLOCKS], outs[BLOCKS : BLOCKS + 3]
        scratch = outs[BLOCKS + 3 :]
    else:
        acc, rest, left = outs[:3]
        scratch = outs[3:]
    xs, ring, slots, table, mine, ring_sem, slot_sem = scratch

    reads = [
        pltpu.make_async_copy(piece.at[pl.ds(BLOCKS * TILE, 8)], slots.at[i], slot_sem.at[i])
        for i, piece in enumerate(pieces)
    ]
    for read in reads:
        read.start()
    for p in range(BUCKETS * BLOCKS):
        table[p] = -1
    for read in reads:
        read.wait()
    for i in range(n_pieces):
        for j in range(BLOCKS):
            table[slots[i, 0, j].astype(jnp.int32) & 127] = i * BLOCKS + j

    def sort(group, n):
        here, there = n
        loaded = [words[group * UNROLL + j] for j in range(UNROLL)]
        found = [table[(word >> 8) & 127] for word in loaded]
        for word, s in zip(loaded, found):
            live = (word >= 0).astype(jnp.int32)
            known = jnp.where(s >= 0, live, 0)
            mine[here] = (word & 0xFF00FF) | (s << 8)
            rest[there] = word
            here, there = here + known, there + live - known
        return here, there

    here, there = lax.fori_loop(0, (count[0] + UNROLL - 1) // UNROLL, sort, (0, 0))
    left[0] = there
    for j in range(UNROLL):
        mine[here + j] = DUMMY * 65536
        rest[there + j] = -1
    groups = (here + UNROLL - 1) // UNROLL

    def fetch(group):
        slot = group % DEPTH
        for j in range(UNROLL):
            at = mine[group * UNROLL + j] & 255
            pltpu.make_async_copy(tiles.at[at], ring.at[slot, j], ring_sem.at[slot, j]).start()

    for group in range(DEPTH - 1):

        @pl.when(group < groups)
        def _(group=group):
            fetch(group)

    def halve(j, carry):
        for i, piece in enumerate(pieces):
            xs[i * BLOCKS + j] = halves(piece[pl.ds(pl.multiple_of(j * TILE, TILE), TILE), :])
        return carry

    lax.fori_loop(0, BLOCKS, halve, 0)

    def begin(d, carry):
        acc[d] = jnp.zeros((TILE, FEAT), f32) if first else so_far[d]
        return carry

    lax.fori_loop(0, DUMMY + 1, begin, 0, unroll=5)

    def step(group, carry):
        @pl.when(group + DEPTH - 1 < groups)
        def _():
            fetch(group + DEPTH - 1)

        slot = group % DEPTH
        own = [mine[group * UNROLL + j] for j in range(UNROLL)]
        for j in range(UNROLL):
            pltpu.make_async_copy(tiles.at[0], ring.at[slot, j], ring_sem.at[slot, j]).wait()
        results = [product(halves(ring[slot, j]), xs[(own[j] >> 8) & 127]) for j in range(UNROLL)]
        for w, result in zip(own, results):
            acc[w >> 16] += result
        return carry

    lax.fori_loop(0, groups, step, 0)
    if last:

        def hand_out(j, carry):
            for i, out in enumerate(parts):
                owner = ((i // 4) ^ place[0]) * 4 + (i % 4 + place[1] & 3)
                out[j] = acc[owner * BLOCKS + j]
            return carry

        lax.fori_loop(0, BLOCKS, hand_out, 0)


def tile_products(place, words, count, tiles, pieces, so_far=None, last=False):
    first = so_far is None
    smem = pl.BlockSpec(memory_space=pltpu.SMEM)
    vmem = pl.BlockSpec(memory_space=pltpu.VMEM)
    hbm = pl.BlockSpec(memory_space=pltpu.HBM)
    sums = pltpu.VMEM((DUMMY + 1, TILE, FEAT), f32)
    going_on = [pltpu.SMEM((TILES + 2 * UNROLL,), jnp.int32), pltpu.SMEM((1,), jnp.int32)]
    part = jax.ShapeDtypeStruct((BLOCKS, TILE, FEAT), f32)
    return pl.pallas_call(
        functools.partial(tile_kernel, len(pieces), first, last),
        out_shape=[part] * BLOCKS
        if last
        else [jax.ShapeDtypeStruct(r.shape, r.dtype) for r in (sums, *going_on)],
        in_specs=[smem, smem, smem, hbm] + [vmem] * (len(pieces) + (not first)),
        out_specs=[vmem] * BLOCKS if last else [vmem, smem, smem],
        scratch_shapes=([sums, *going_on] if last else [])
        + [
            pltpu.VMEM((len(pieces) * BLOCKS, TILE, 2 * FEAT), bf16),
            pltpu.VMEM((DEPTH, UNROLL, TILE, TILE), f32),
            pltpu.SMEM((len(pieces), 8, 128), f32),
            pltpu.SMEM((BUCKETS * BLOCKS,), jnp.int32),
            pltpu.SMEM((TILES + 2 * UNROLL,), jnp.int32),
            pltpu.SemaphoreType.DMA((DEPTH, UNROLL)),
            pltpu.SemaphoreType.DMA((len(pieces),)),
        ],
        compiler_params=pltpu.CompilerParams(vmem_limit_bytes=40 * 2**20),
        cost_estimate=pl.CostEstimate(flops=10**5, bytes_accessed=10**4, transcendentals=0),
    )(place, words, count, tiles, *pieces, *([] if first else [so_far]))


def finish_kernel(a, b, c, d, weight, bias, out):
    total = a[...] + b[...] + c[...] + d[...]
    hidden = product(halves(total.reshape(BLOCKS * TILE, FEAT)), halves(weight[...]))
    out[...] = jnp.maximum(hidden + bias[...], 0.0)


def after(value, *others):
    return lax.optimization_barrier((value, *others))[0]


def body(features, new_slot, tile_values, tile_dest, tile_source, weight, bias_vector):
    move = lax.ppermute
    row = jnp.pad(new_slot.astype(f32)[None, :], ((0, 7), (0, FEAT - BLOCKS)))
    own = jnp.concatenate([features, row])
    below = move(own, "y", UP)
    above = move(own, "y", DOWN)
    far = move(own, "z_hi", SWAP)
    other = move(own, "core", SWAP)

    place = jnp.stack([lax.axis_index("z_lo"), lax.axis_index("x")]).astype(jnp.int32)
    tiles = tile_values.reshape(TILES, TILE, TILE)
    smem = pl.BlockSpec(memory_space=pltpu.SMEM)
    words, count = pl.pallas_call(
        live_kernel,
        out_shape=[
            jax.ShapeDtypeStruct((TILES + 2 * UNROLL,), jnp.int32),
            jax.ShapeDtypeStruct((1,), jnp.int32),
        ],
        in_specs=[smem, smem],
        out_specs=[smem, smem],
        cost_estimate=pl.CostEstimate(flops=10**5, bytes_accessed=10**4, transcendentals=0),
    )(tile_dest.reshape(BUCKETS, SLOTS), tile_source.reshape(BUCKETS, SLOTS))

    below = after(below, words)
    two = move(below, "y", UP)
    far_above = move(far, "y", DOWN)
    far_below = move(below, "z_hi", SWAP)
    swapped = [move(p, "core", SWAP) for p in (below, above, far)]
    sums, words, count = tile_products(place, words, count, tiles, [own, other, below, above, far, *swapped])

    two = after(two, sums)
    far_two = move(two, "z_hi", SWAP)
    late = [two, far_above, far_below]
    swapped = [move(p, "core", SWAP) for p in late]
    sums, words, count = tile_products(place, words, count, tiles, late, sums)

    far_two = after(far_two, sums)
    mine, up, two, down, z_mine, z_up, z_two, z_down = tile_products(
        place, words, count, tiles, [*swapped, far_two, move(far_two, "core", SWAP)], sums, last=True
    )

    half = BLOCKS // 2
    got_two = move(z_two, "z_lo", SWAP)
    got_up = move(z_up, "x", UP)
    got_down = move(z_down, "x", DOWN)
    two_up = move(two[:half] + got_two[:half], "x", UP)
    two_down = move(two[half:] + got_two[half:], "x", DOWN)
    end_z = move(z_mine + got_up + got_down, "z_lo", SWAP)
    end_up = move(jnp.concatenate([up[:half] + two_up, up[half:]]), "x", UP)
    end_down = move(jnp.concatenate([down[:half], down[half:] + two_down]), "x", DOWN)

    return pl.pallas_call(
        finish_kernel,
        out_shape=jax.ShapeDtypeStruct((BLOCKS * TILE, FEAT), f32),
        compiler_params=pltpu.CompilerParams(vmem_limit_bytes=24 * 2**20),
    )(mine, end_up, end_down, end_z, weight, bias_vector.reshape(1, FEAT))


def solution(mesh):
    fine = Mesh(mesh.devices.reshape(2, 4, 2, 4, 2), AXES)
    grp, blk = AXES[:2], AXES[2:]
    return jax.shard_map(
        body,
        mesh=fine,
        in_specs=(
            P(AXES, None),
            P(AXES),
            P(grp, blk, None, None, None, None),
            P(grp, blk, None, None),
            P(grp, blk, None, None),
            P(),
            P(),
        ),
        out_specs=P(AXES, None),
        check_vma=False,
    )
```

```python
import functools

import jax
import jax.numpy as jnp
from jax import lax
from jax.experimental import pallas as pl
from jax.experimental.pallas import tpu as pltpu
from jax.sharding import Mesh, PartitionSpec as P

TILE = 128
FEAT = 128
BLOCKS = 8
SLOTS = 16
BUCKETS = 16
TILES = BUCKETS * SLOTS
STEP = 16
LAST_STEP = 8
RING = 48
DUMMY = 64

AXES = ("z_lo", "x", "z_hi", "y", "core")
UP = [(i, (i + 1) % 4) for i in range(4)]
DOWN = [(i, (i - 1) % 4) for i in range(4)]
SWAP = [(0, 1), (1, 0)]

f32, bf16 = jnp.float32, jnp.bfloat16


def split(v):
    hi = v.astype(bf16)
    return hi, (v - hi.astype(f32)).astype(bf16)


def halves(v):
    return jnp.concatenate(split(v), axis=1)


def product(left, right):
    both = jnp.dot(left, jnp.concatenate([right, right], axis=0), preferred_element_type=f32)
    return both[:, :FEAT] + both[:, FEAT:]


def live_kernel(dest, source, words, count):
    def bucket(k, n):
        loaded = [(dest[k, t], source[k, t]) for t in range(SLOTS)]
        for t, (d, s) in enumerate(loaded):
            words[n] = (k * SLOTS + t) + (k * BLOCKS + s) * 256 + d * 65536
            n = n + (d >= 0).astype(jnp.int32)
        return n

    total = lax.fori_loop(0, BUCKETS, bucket, 0)
    count[0] = total
    for j in range(STEP):
        words[total + j] = -1


def tile_kernel(n_pieces, first, last, *refs):
    place, words, count, tiles = refs[:4]
    refs = refs[1:]
    pieces = refs[3 : 3 + n_pieces]
    so_far = None if first else refs[3 + n_pieces]
    outs = refs[4 + n_pieces - first :]
    if last:
        parts, (acc, *scratch) = outs[:BLOCKS], outs[BLOCKS:]
    else:
        acc, rest, left, mine, *scratch = outs
    xs, ring, slots, table, ring_sem, slot_sem = scratch
    size = LAST_STEP if last else STEP
    depth = RING // size

    reads = [
        pltpu.make_async_copy(piece.at[pl.ds(BLOCKS * TILE, 8)], slots.at[i], slot_sem.at[i])
        for i, piece in enumerate(pieces)
    ]
    for read in reads:
        read.start()

    def fetch(group):
        slot = group % depth
        for j in range(size):
            pltpu.make_async_copy(
                tiles.at[todo[group * size + j] & 255], ring.at[slot, j], ring_sem.at[slot, j]
            ).start()

    def fetch_first():
        for group in range(depth - 1):

            @pl.when(group < groups)
            def _(group=group):
                fetch(group)

    if last:
        todo, here = words, count[0]
        groups = (here + size - 1) // size
        fetch_first()
    else:
        for p in range(BUCKETS * BLOCKS):
            table[p] = -1

    def begin(d, carry):
        acc[d] = jnp.zeros((TILE, FEAT), f32) if first else so_far[d]
        return carry

    lax.fori_loop(0, DUMMY + 1, begin, 0, unroll=5)
    for read in reads:
        read.wait()
    for i in range(n_pieces):
        for j in range(BLOCKS):
            table[slots[i, 0, j].astype(jnp.int32) & 127] = i * BLOCKS + j

    def sort(group, n):
        here, there = n
        loaded = [words[group * 8 + j] for j in range(8)]
        found = [table[(word >> 8) & 127] for word in loaded]
        for word, s in zip(loaded, found):
            live = (word >= 0).astype(jnp.int32)
            known = jnp.where(s >= 0, live, 0)
            mine[here] = word
            rest[there] = word
            here, there = here + known, there + live - known
        return here, there

    if not last:
        here, there = lax.fori_loop(0, (count[0] + 7) // 8, sort, (0, 0))
        left[0] = there
        for j in range(STEP):
            mine[here + j] = -1
            rest[there + j] = -1
        todo, groups = mine, (here + size - 1) // size
        fetch_first()

    def halve(j, carry):
        for i, piece in enumerate(pieces):
            xs[i * BLOCKS + j] = halves(piece[pl.ds(pl.multiple_of(j * TILE, TILE), TILE), :])
        return carry

    lax.fori_loop(0, BLOCKS, halve, 0)

    def step(group, carry):
        @pl.when(group + depth - 1 < groups)
        def _():
            fetch(group + depth - 1)

        slot = group % depth
        own = [todo[group * size + j] for j in range(size)]
        live = [w >= 0 for w in own]
        source = [jnp.where(l, table[(w >> 8) & 127], 0) for w, l in zip(own, live)]
        target = [jnp.where(l, w >> 16, DUMMY) for w, l in zip(own, live)]
        for j in range(size):
            pltpu.make_async_copy(tiles.at[0], ring.at[slot, j], ring_sem.at[slot, j]).wait()
        results = [product(halves(ring[slot, j]), xs[source[j]]) for j in range(size)]
        for d, result in zip(target, results):
            acc[d] += result
        return carry

    lax.fori_loop(0, groups, step, 0)
    if last:

        def hand_out(j, carry):
            for i, out in enumerate(parts):
                owner = ((i // 4) ^ place[0]) * 4 + (i % 4 + place[1] & 3)
                out[j] = acc[owner * BLOCKS + j]
            return carry

        lax.fori_loop(0, BLOCKS, hand_out, 0)


def tile_products(place, words, count, tiles, pieces, so_far=None, last=False):
    first = so_far is None
    size = LAST_STEP if last else STEP
    smem = pl.BlockSpec(memory_space=pltpu.SMEM)
    vmem = pl.BlockSpec(memory_space=pltpu.VMEM)
    hbm = pl.BlockSpec(memory_space=pltpu.HBM)
    sums = pltpu.VMEM((DUMMY + 1, TILE, FEAT), f32)
    going_on = [pltpu.SMEM((TILES + 2 * STEP,), jnp.int32), pltpu.SMEM((1,), jnp.int32)]
    part = jax.ShapeDtypeStruct((BLOCKS, TILE, FEAT), f32)
    return pl.pallas_call(
        functools.partial(tile_kernel, len(pieces), first, last),
        out_shape=[part] * BLOCKS
        if last
        else [jax.ShapeDtypeStruct(r.shape, r.dtype) for r in (sums, *going_on)],
        in_specs=[smem, smem, smem, hbm] + [vmem] * (len(pieces) + (not first)),
        out_specs=[vmem] * BLOCKS if last else [vmem, smem, smem],
        scratch_shapes=[sums if last else going_on[0]]
        + [
            pltpu.VMEM((len(pieces) * BLOCKS, TILE, 2 * FEAT), bf16),
            pltpu.VMEM((RING // size, size, TILE, TILE), f32),
            pltpu.SMEM((len(pieces), 8, 128), f32),
            pltpu.SMEM((BUCKETS * BLOCKS,), jnp.int32),
            pltpu.SemaphoreType.DMA((RING // size, size)),
            pltpu.SemaphoreType.DMA((len(pieces),)),
        ],
        compiler_params=pltpu.CompilerParams(vmem_limit_bytes=40 * 2**20),
        cost_estimate=pl.CostEstimate(flops=10**5, bytes_accessed=10**4, transcendentals=0),
    )(place, words, count, tiles, *pieces, *([] if first else [so_far]))


def finish_kernel(a, b, c, d, weight, bias, out):
    total = a[...] + b[...] + c[...] + d[...]
    hidden = product(halves(total.reshape(BLOCKS * TILE, FEAT)), halves(weight[...]))
    out[...] = jnp.maximum(hidden + bias[...], 0.0)


def after(value, *others):
    return lax.optimization_barrier((value, *others))[0]


def body(features, new_slot, tile_values, tile_dest, tile_source, weight, bias_vector):
    move = lax.ppermute
    row = jnp.pad(new_slot.astype(f32)[None, :], ((0, 7), (0, FEAT - BLOCKS)))
    own = jnp.concatenate([features, row])
    below = move(own, "y", UP)
    above = move(own, "y", DOWN)
    far = move(own, "z_hi", SWAP)
    other = move(own, "core", SWAP)

    place = jnp.stack([lax.axis_index("z_lo"), lax.axis_index("x")]).astype(jnp.int32)
    tiles = tile_values.reshape(TILES, TILE, TILE)
    smem = pl.BlockSpec(memory_space=pltpu.SMEM)
    words, count = pl.pallas_call(
        live_kernel,
        out_shape=[
            jax.ShapeDtypeStruct((TILES + 2 * STEP,), jnp.int32),
            jax.ShapeDtypeStruct((1,), jnp.int32),
        ],
        in_specs=[smem, smem],
        out_specs=[smem, smem],
        cost_estimate=pl.CostEstimate(flops=10**5, bytes_accessed=10**4, transcendentals=0),
    )(tile_dest.reshape(BUCKETS, SLOTS), tile_source.reshape(BUCKETS, SLOTS))

    below = after(below, words)
    two = move(below, "y", UP)
    far_above = move(far, "y", DOWN)
    far_below = move(below, "z_hi", SWAP)
    swapped = [move(p, "core", SWAP) for p in (below, above, far)]
    far_two = move(two, "z_hi", SWAP)
    late = [two, far_above, far_below]
    late_swapped = [move(p, "core", SWAP) for p in late]
    early = [own, other, below, above, far, *swapped, *late]
    sums, words, count = tile_products(place, words, count, tiles, early)
    far_two = after(far_two, sums)
    mine, up, two, down, z_mine, z_up, z_two, z_down = tile_products(
        place, words, count, tiles, [*late_swapped, far_two, move(far_two, "core", SWAP)], sums, last=True
    )

    half = BLOCKS // 2
    got_two = move(z_two, "z_lo", SWAP)
    got_up = move(z_up, "x", UP)
    got_down = move(z_down, "x", DOWN)
    two_up = move(two[:half] + got_two[:half], "x", UP)
    two_down = move(two[half:] + got_two[half:], "x", DOWN)
    end_z = move(z_mine + got_up + got_down, "z_lo", SWAP)
    end_up = move(jnp.concatenate([up[:half] + two_up, up[half:]]), "x", UP)
    end_down = move(jnp.concatenate([down[:half], down[half:] + two_down]), "x", DOWN)

    return pl.pallas_call(
        finish_kernel,
        out_shape=jax.ShapeDtypeStruct((BLOCKS * TILE, FEAT), f32),
        compiler_params=pltpu.CompilerParams(vmem_limit_bytes=24 * 2**20),
    )(mine, end_up, end_down, end_z, weight, bias_vector.reshape(1, FEAT))


def solution(mesh):
    fine = Mesh(mesh.devices.reshape(2, 4, 2, 4, 2), AXES)
    grp, blk = AXES[:2], AXES[2:]
    return jax.shard_map(
        body,
        mesh=fine,
        in_specs=(
            P(AXES, None),
            P(AXES),
            P(grp, blk, None, None, None, None),
            P(grp, blk, None, None),
            P(grp, blk, None, None),
            P(),
            P(),
        ),
        out_specs=P(AXES, None),
        check_vma=False,
    )
```

```python
import functools

import jax
import jax.numpy as jnp
from jax import lax
from jax.experimental import pallas as pl
from jax.experimental.pallas import tpu as pltpu
from jax.sharding import Mesh, PartitionSpec as P

TILE = 128
FEAT = 128
BLOCKS = 8
SLOTS = 16
BUCKETS = 16
TILES = BUCKETS * SLOTS
STEP = 16
LAST_STEP = 8
RING = 48
DUMMY = 64

AXES = ("z_lo", "x", "z_hi", "y", "core")
UP = [(i, (i + 1) % 4) for i in range(4)]
DOWN = [(i, (i - 1) % 4) for i in range(4)]
SWAP = [(0, 1), (1, 0)]

f32, bf16 = jnp.float32, jnp.bfloat16


def split(v):
    hi = v.astype(bf16)
    return hi, (v - hi.astype(f32)).astype(bf16)


def halves(v):
    return jnp.concatenate(split(v), axis=1)


def product(left, right):
    both = jnp.dot(left, jnp.concatenate([right, right], axis=0), preferred_element_type=f32)
    return both[:, :FEAT] + both[:, FEAT:]


def live_kernel(dest, source, words, count):
    def bucket(k, n):
        loaded = [(dest[k, t], source[k, t]) for t in range(SLOTS)]
        for t, (d, s) in enumerate(loaded):
            words[n] = (k * SLOTS + t) + (k * BLOCKS + s) * 256 + d * 65536
            n = n + (d >= 0).astype(jnp.int32)
        return n

    total = lax.fori_loop(0, BUCKETS, bucket, 0)
    count[0] = total
    for j in range(STEP):
        words[total + j] = -1


def tile_kernel(n_pieces, first, split_rest, owners, *refs):
    place, words, count, tiles = refs[:4]
    refs = refs[4:]
    pieces, refs = refs[:n_pieces], refs[n_pieces:]
    so_far = None if first else refs[0]
    outs = refs[1 - first :]
    if owners:
        parts, (acc, *scratch) = outs[: len(owners)], outs[len(owners) :]
        dummy, size = len(owners) * BLOCKS, LAST_STEP
    else:
        acc, *outs = outs
        rests, (mine, *scratch) = outs[: 2 + 2 * split_rest], outs[2 + 2 * split_rest :]
        dummy, size = DUMMY, STEP
    xs, ring, slots, table, ring_sem, slot_sem = scratch
    depth = RING // size

    reads = [
        pltpu.make_async_copy(piece.at[pl.ds(BLOCKS * TILE, 8)], slots.at[i], slot_sem.at[i])
        for i, piece in enumerate(pieces)
    ]
    for read in reads:
        read.start()

    def fetch(group):
        slot = group % depth
        for j in range(size):
            pltpu.make_async_copy(
                tiles.at[todo[group * size + j] & 255], ring.at[slot, j], ring_sem.at[slot, j]
            ).start()

    def fetch_first():
        for group in range(depth - 1):

            @pl.when(group < groups)
            def _(group=group):
                fetch(group)

    if owners:
        todo, groups = words, (count[0] + size - 1) // size
        fetch_first()

        def begin(j, carry):
            for i, owner in enumerate(owners):
                at = ((owner // 4) ^ place[0]) * 4 + (owner % 4 + place[1] & 3)
                acc[i * BLOCKS + j] = so_far[at * BLOCKS + j]
            return carry

        lax.fori_loop(0, BLOCKS, begin, 0)
    else:
        for p in range(BUCKETS * BLOCKS):
            table[p] = -1

        def begin(d, carry):
            acc[d] = jnp.zeros((TILE, FEAT), f32) if first else so_far[d]
            return carry

        lax.fori_loop(0, DUMMY + 1, begin, 0, unroll=5)
    for read in reads:
        read.wait()
    for i in range(n_pieces):
        for j in range(BLOCKS):
            table[slots[i, 0, j].astype(jnp.int32) & 127] = i * BLOCKS + j

    def sort(group, n):
        here, *others = n
        loaded = [words[group * 8 + j] for j in range(8)]
        found = [table[(word >> 8) & 127] for word in loaded]
        for word, s in zip(loaded, found):
            live = (word >= 0).astype(jnp.int32)
            known = jnp.where(s >= 0, live, 0)
            mine[here] = word
            here = here + known
            left = [live - known]
            if split_rest:
                g = word >> 19
                soon = jnp.where((g & 3) != place[1], (g >> 2) ^ place[0], 0) * left[0]
                left = [soon, left[0] - soon]
            for i, more in enumerate(left):
                rests[2 * i][others[i]] = word
                others[i] = others[i] + more
        return (here, *others)

    if not owners:
        here, *others = lax.fori_loop(0, (count[0] + 7) // 8, sort, (0,) * (2 + split_rest))
        for j in range(STEP):
            mine[here + j] = -1
        for i, n in enumerate(others):
            rests[2 * i + 1][0] = n
            for j in range(STEP):
                rests[2 * i][n + j] = -1
        todo, groups = mine, (here + size - 1) // size
        fetch_first()

    def halve(j, carry):
        for i, piece in enumerate(pieces):
            xs[i * BLOCKS + j] = halves(piece[pl.ds(pl.multiple_of(j * TILE, TILE), TILE), :])
        return carry

    lax.fori_loop(0, BLOCKS, halve, 0)

    def goal(word):
        if not owners:
            return word >> 16
        g = word >> 19
        distance = ((g >> 2) ^ place[0]) * 4 + ((g & 3) - place[1] & 3)
        return (distance - owners[0]) * BLOCKS + ((word >> 16) & 7)

    def step(group, carry):
        @pl.when(group + depth - 1 < groups)
        def _():
            fetch(group + depth - 1)

        slot = group % depth
        own = [todo[group * size + j] for j in range(size)]
        live = [w >= 0 for w in own]
        source = [jnp.where(l, table[(w >> 8) & 127], 0) for w, l in zip(own, live)]
        target = [jnp.where(l, goal(w), dummy) for w, l in zip(own, live)]
        for j in range(size):
            pltpu.make_async_copy(tiles.at[0], ring.at[slot, j], ring_sem.at[slot, j]).wait()
        results = [product(halves(ring[slot, j]), xs[source[j]]) for j in range(size)]
        for d, result in zip(target, results):
            acc[d] += result
        return carry

    lax.fori_loop(0, groups, step, 0)
    if owners:

        def hand_out(j, carry):
            for i, out in enumerate(parts):
                out[j] = acc[i * BLOCKS + j]
            return carry

        lax.fori_loop(0, BLOCKS, hand_out, 0)


def tile_products(place, words, count, tiles, pieces, so_far=None, split_rest=False, owners=()):
    first = so_far is None
    size = LAST_STEP if owners else STEP
    smem = pl.BlockSpec(memory_space=pltpu.SMEM)
    vmem = pl.BlockSpec(memory_space=pltpu.VMEM)
    hbm = pl.BlockSpec(memory_space=pltpu.HBM)
    listed = [pltpu.SMEM((TILES + 2 * STEP,), jnp.int32), pltpu.SMEM((1,), jnp.int32)]
    rests = listed * (1 + split_rest)
    part = jax.ShapeDtypeStruct((BLOCKS, TILE, FEAT), f32)
    sums = pltpu.VMEM(((len(owners) * BLOCKS or DUMMY) + 1, TILE, FEAT), f32)
    return pl.pallas_call(
        functools.partial(tile_kernel, len(pieces), first, split_rest, owners),
        out_shape=[part] * len(owners)
        or [jax.ShapeDtypeStruct(r.shape, r.dtype) for r in (sums, *rests)],
        in_specs=[smem, smem, smem, hbm] + [vmem] * (len(pieces) + (not first)),
        out_specs=[vmem] * len(owners) or [vmem] + [smem] * len(rests),
        scratch_shapes=[sums if owners else listed[0]]
        + [
            pltpu.VMEM((len(pieces) * BLOCKS, TILE, 2 * FEAT), bf16),
            pltpu.VMEM((RING // size, size, TILE, TILE), f32),
            pltpu.SMEM((len(pieces), 8, 128), f32),
            pltpu.SMEM((BUCKETS * BLOCKS,), jnp.int32),
            pltpu.SemaphoreType.DMA((RING // size, size)),
            pltpu.SemaphoreType.DMA((len(pieces),)),
        ],
        compiler_params=pltpu.CompilerParams(vmem_limit_bytes=40 * 2**20),
        cost_estimate=pl.CostEstimate(flops=10**5, bytes_accessed=10**4, transcendentals=0),
    )(place, words, count, tiles, *pieces, *([] if first else [so_far]))


def finish_kernel(a, b, c, d, weight, bias, out):
    total = a[...] + b[...] + c[...] + d[...]
    hidden = product(halves(total.reshape(BLOCKS * TILE, FEAT)), halves(weight[...]))
    out[...] = jnp.maximum(hidden + bias[...], 0.0)


def after(value, *others):
    return lax.optimization_barrier((value, *others))[0]


def body(features, new_slot, tile_values, tile_dest, tile_source, weight, bias_vector):
    move = lax.ppermute
    row = jnp.pad(new_slot.astype(f32)[None, :], ((0, 7), (0, FEAT - BLOCKS)))
    own = jnp.concatenate([features, row])
    below = move(own, "y", UP)
    above = move(own, "y", DOWN)
    far = move(own, "z_hi", SWAP)
    other = move(own, "core", SWAP)

    place = jnp.stack([lax.axis_index("z_lo"), lax.axis_index("x")]).astype(jnp.int32)
    tiles = tile_values.reshape(TILES, TILE, TILE)
    smem = pl.BlockSpec(memory_space=pltpu.SMEM)
    words, count = pl.pallas_call(
        live_kernel,
        out_shape=[
            jax.ShapeDtypeStruct((TILES + 2 * STEP,), jnp.int32),
            jax.ShapeDtypeStruct((1,), jnp.int32),
        ],
        in_specs=[smem, smem],
        out_specs=[smem, smem],
        cost_estimate=pl.CostEstimate(flops=10**5, bytes_accessed=10**4, transcendentals=0),
    )(tile_dest.reshape(BUCKETS, SLOTS), tile_source.reshape(BUCKETS, SLOTS))

    below = after(below, words)
    two = move(below, "y", UP)
    far_above = move(far, "y", DOWN)
    far_below = move(below, "z_hi", SWAP)
    swapped = [move(p, "core", SWAP) for p in (below, above, far)]
    sums, words, count = tile_products(place, words, count, tiles, [own, other, below, above, far])

    two = after(two, sums)
    far_two = move(two, "z_hi", SWAP)
    late = [two, far_above, far_below]
    late_swapped = [move(p, "core", SWAP) for p in late]
    sums, soon, n_soon, words, count = tile_products(
        place, words, count, tiles, [*swapped, *late], sums, split_rest=True
    )

    far_two = after(far_two, sums)
    last = [*late_swapped, far_two, move(far_two, "core", SWAP)]
    z_up, z_two, z_down = tile_products(place, soon, n_soon, tiles, last, sums, owners=(5, 6, 7))
    mine, up, two, down, z_mine = tile_products(
        place, words, count, tiles, last, after(sums, z_two), owners=(0, 1, 2, 3, 4)
    )

    half = BLOCKS // 2
    got_two = move(z_two, "z_lo", SWAP)
    got_up = move(z_up, "x", UP)
    got_down = move(z_down, "x", DOWN)
    two_up = move(two[:half] + got_two[:half], "x", UP)
    two_down = move(two[half:] + got_two[half:], "x", DOWN)
    end_z = move(z_mine + got_up + got_down, "z_lo", SWAP)
    end_up = move(jnp.concatenate([up[:half] + two_up, up[half:]]), "x", UP)
    end_down = move(jnp.concatenate([down[:half], down[half:] + two_down]), "x", DOWN)

    return pl.pallas_call(
        finish_kernel,
        out_shape=jax.ShapeDtypeStruct((BLOCKS * TILE, FEAT), f32),
        compiler_params=pltpu.CompilerParams(vmem_limit_bytes=24 * 2**20),
    )(mine, end_up, end_down, end_z, weight, bias_vector.reshape(1, FEAT))


def solution(mesh):
    fine = Mesh(mesh.devices.reshape(2, 4, 2, 4, 2), AXES)
    grp, blk = AXES[:2], AXES[2:]
    return jax.shard_map(
        body,
        mesh=fine,
        in_specs=(
            P(AXES, None),
            P(AXES),
            P(grp, blk, None, None, None, None),
            P(grp, blk, None, None),
            P(grp, blk, None, None),
            P(),
            P(),
        ),
        out_specs=P(AXES, None),
        check_vma=False,
    )
```

```python
import functools

import jax
import jax.numpy as jnp
from jax import lax
from jax.experimental import pallas as pl
from jax.experimental.pallas import tpu as pltpu
from jax.sharding import Mesh, PartitionSpec as P

TILE = 128
FEAT = 128
BLOCKS = 8
HALF = 4
SLOTS = 16
BUCKETS = 16
TILES = BUCKETS * SLOTS
STEP = 16
LAST_STEP = 8
RING = 48
DUMMY = 64

AXES = ("z_lo", "x", "z_hi", "y", "core")
UP = [(i, (i + 1) % 4) for i in range(4)]
DOWN = [(i, (i - 1) % 4) for i in range(4)]
SWAP = [(0, 1), (1, 0)]

f32, bf16 = jnp.float32, jnp.bfloat16


def split(v):
    hi = v.astype(bf16)
    return hi, (v - hi.astype(f32)).astype(bf16)


def halves(v):
    return jnp.concatenate(split(v), axis=1)


def product(left, right):
    both = jnp.dot(left, jnp.concatenate([right, right], axis=0), preferred_element_type=f32)
    return both[:, :FEAT] + both[:, FEAT:]


def live_kernel(dest, source, words, count):
    def bucket(k, n):
        loaded = [(dest[k, t], source[k, t]) for t in range(SLOTS)]
        for t, (d, s) in enumerate(loaded):
            words[n] = (k * SLOTS + t) + (k * BLOCKS + s) * 256 + d * 65536
            n = n + (d >= 0).astype(jnp.int32)
        return n

    total = lax.fori_loop(0, BUCKETS, bucket, 0)
    count[0] = total
    for j in range(STEP):
        words[total + j] = -1


def tile_kernel(n_pieces, first, split_rest, owners, halved, *refs):
    place, words, count, tiles = refs[:4]
    refs = refs[4:]
    pieces, refs = refs[:n_pieces], refs[n_pieces:]
    so_far = None if first else refs[0]
    outs = refs[1 - first :]
    if owners:
        n_parts = len(owners) + len(halved)
        parts, (acc, *scratch) = outs[:n_parts], outs[n_parts:]
        dummy, size = len(owners) * BLOCKS, LAST_STEP
    else:
        acc, *outs = outs
        rests, (mine, *scratch) = outs[: 2 + 2 * split_rest], outs[2 + 2 * split_rest :]
        dummy, size = DUMMY, STEP
    xs, ring, slots, table, ring_sem, slot_sem = scratch
    depth = RING // size

    reads = [
        pltpu.make_async_copy(piece.at[pl.ds(BLOCKS * TILE, 8)], slots.at[i], slot_sem.at[i])
        for i, piece in enumerate(pieces)
    ]
    for read in reads:
        read.start()

    def fetch(group):
        slot = group % depth
        for j in range(size):
            pltpu.make_async_copy(
                tiles.at[todo[group * size + j] & 255], ring.at[slot, j], ring_sem.at[slot, j]
            ).start()

    def fetch_first():
        for group in range(depth - 1):

            @pl.when(group < groups)
            def _(group=group):
                fetch(group)

    if owners:
        todo, groups = words, (count[0] + size - 1) // size
        fetch_first()

        def begin(j, carry):
            for i, owner in enumerate(owners):
                at = ((owner // 4) ^ place[0]) * 4 + (owner % 4 + place[1] & 3)
                acc[i * BLOCKS + j] = so_far[at * BLOCKS + j]
            return carry

        lax.fori_loop(0, BLOCKS, begin, 0)
    else:
        for p in range(BUCKETS * BLOCKS):
            table[p] = -1

        def begin(d, carry):
            acc[d] = jnp.zeros((TILE, FEAT), f32) if first else so_far[d]
            return carry

        lax.fori_loop(0, DUMMY + 1, begin, 0, unroll=5)
    for read in reads:
        read.wait()
    for i in range(n_pieces):
        for j in range(BLOCKS):
            table[slots[i, 0, j].astype(jnp.int32) & 127] = i * BLOCKS + j

    def sort(group, n):
        here, *others = n
        loaded = [words[group * 8 + j] for j in range(8)]
        found = [table[(word >> 8) & 127] for word in loaded]
        for word, s in zip(loaded, found):
            live = (word >= 0).astype(jnp.int32)
            known = jnp.where(s >= 0, live, 0)
            mine[here] = word
            here = here + known
            left = [live - known]
            if split_rest:
                g = word >> 19
                soon = jnp.where((g & 3) != place[1], (g >> 2) ^ place[0], 0) * left[0]
                left = [soon, left[0] - soon]
            for i, more in enumerate(left):
                rests[2 * i][others[i]] = word
                others[i] = others[i] + more
        return (here, *others)

    if not owners:
        here, *others = lax.fori_loop(0, (count[0] + 7) // 8, sort, (0,) * (2 + split_rest))
        for j in range(STEP):
            mine[here + j] = -1
        for i, n in enumerate(others):
            rests[2 * i + 1][0] = n
            for j in range(STEP):
                rests[2 * i][n + j] = -1
        todo, groups = mine, (here + size - 1) // size
        fetch_first()

    def halve(j, carry):
        for i, piece in enumerate(pieces):
            xs[i * BLOCKS + j] = halves(piece[pl.ds(pl.multiple_of(j * TILE, TILE), TILE), :])
        return carry

    lax.fori_loop(0, BLOCKS, halve, 0)

    def goal(word):
        if not owners:
            return word >> 16
        g = word >> 19
        distance = ((g >> 2) ^ place[0]) * 4 + ((g & 3) - place[1] & 3)
        return (distance - owners[0]) * BLOCKS + ((word >> 16) & 7)

    def step(group, carry):
        @pl.when(group + depth - 1 < groups)
        def _():
            fetch(group + depth - 1)

        slot = group % depth
        own = [todo[group * size + j] for j in range(size)]
        live = [w >= 0 for w in own]
        source = [jnp.where(l, table[(w >> 8) & 127], 0) for w, l in zip(own, live)]
        target = [jnp.where(l, goal(w), dummy) for w, l in zip(own, live)]
        for j in range(size):
            pltpu.make_async_copy(tiles.at[0], ring.at[slot, j], ring_sem.at[slot, j]).wait()
        results = [product(halves(ring[slot, j]), xs[source[j]]) for j in range(size)]
        for d, result in zip(target, results):
            acc[d] += result
        return carry

    lax.fori_loop(0, groups, step, 0)
    if owners:

        def hand_out(j, carry):
            at = 0
            for out in parts:
                for part in range(out.shape[0] // HALF):
                    out[part * HALF + j] = acc[at + j]
                    at += HALF
            return carry

        lax.fori_loop(0, HALF, hand_out, 0)


def tile_products(place, words, count, tiles, pieces, so_far=None, split_rest=False, owners=(), halved=()):
    first = so_far is None
    size = LAST_STEP if owners else STEP
    smem = pl.BlockSpec(memory_space=pltpu.SMEM)
    vmem = pl.BlockSpec(memory_space=pltpu.VMEM)
    hbm = pl.BlockSpec(memory_space=pltpu.HBM)
    listed = [pltpu.SMEM((TILES + 2 * STEP,), jnp.int32), pltpu.SMEM((1,), jnp.int32)]
    rests = listed * (1 + split_rest)
    sizes = [n for o in owners for n in ([HALF, HALF] if o in halved else [BLOCKS])]
    parts = [jax.ShapeDtypeStruct((n, TILE, FEAT), f32) for n in sizes]
    sums = pltpu.VMEM(((len(owners) * BLOCKS or DUMMY) + 1, TILE, FEAT), f32)
    return pl.pallas_call(
        functools.partial(tile_kernel, len(pieces), first, split_rest, owners, halved),
        out_shape=parts
        or [jax.ShapeDtypeStruct(r.shape, r.dtype) for r in (sums, *rests)],
        in_specs=[smem, smem, smem, hbm] + [vmem] * (len(pieces) + (not first)),
        out_specs=[vmem] * len(parts) or [vmem] + [smem] * len(rests),
        scratch_shapes=[sums if owners else listed[0]]
        + [
            pltpu.VMEM((len(pieces) * BLOCKS, TILE, 2 * FEAT), bf16),
            pltpu.VMEM((RING // size, size, TILE, TILE), f32),
            pltpu.SMEM((len(pieces), 8, 128), f32),
            pltpu.SMEM((BUCKETS * BLOCKS,), jnp.int32),
            pltpu.SemaphoreType.DMA((RING // size, size)),
            pltpu.SemaphoreType.DMA((len(pieces),)),
        ],
        compiler_params=pltpu.CompilerParams(vmem_limit_bytes=40 * 2**20),
        cost_estimate=pl.CostEstimate(flops=10**5, bytes_accessed=10**4, transcendentals=0),
    )(place, words, count, tiles, *pieces, *([] if first else [so_far]))


def finish_kernel(own, far, up_a, up_b, down_a, down_b, weight, bias, out):
    for half, (up, down) in enumerate(((up_a, down_a), (up_b, down_b))):
        rows = pl.ds(half * HALF, HALF)
        total = (own[rows] + far[rows] + up[...] + down[...]).reshape(HALF * TILE, FEAT)
        hidden = product(halves(total), halves(weight[...]))
        out[pl.ds(half * HALF * TILE, HALF * TILE), :] = jnp.maximum(hidden + bias[...], 0.0)


def after(value, *others):
    return lax.optimization_barrier((value, *others))[0]


def body(features, new_slot, tile_values, tile_dest, tile_source, weight, bias_vector):
    move = lax.ppermute
    row = jnp.pad(new_slot.astype(f32)[None, :], ((0, 7), (0, FEAT - BLOCKS)))
    own = jnp.concatenate([features, row])
    below = move(own, "y", UP)
    above = move(own, "y", DOWN)
    far = move(own, "z_hi", SWAP)
    other = move(own, "core", SWAP)

    place = jnp.stack([lax.axis_index("z_lo"), lax.axis_index("x")]).astype(jnp.int32)
    tiles = tile_values.reshape(TILES, TILE, TILE)
    smem = pl.BlockSpec(memory_space=pltpu.SMEM)
    words, count = pl.pallas_call(
        live_kernel,
        out_shape=[
            jax.ShapeDtypeStruct((TILES + 2 * STEP,), jnp.int32),
            jax.ShapeDtypeStruct((1,), jnp.int32),
        ],
        in_specs=[smem, smem],
        out_specs=[smem, smem],
        cost_estimate=pl.CostEstimate(flops=10**5, bytes_accessed=10**4, transcendentals=0),
    )(tile_dest.reshape(BUCKETS, SLOTS), tile_source.reshape(BUCKETS, SLOTS))

    below = after(below, words)
    two = move(below, "y", UP)
    far_above = move(far, "y", DOWN)
    far_below = move(below, "z_hi", SWAP)
    swapped = [move(p, "core", SWAP) for p in (below, above, far)]
    sums, words, count = tile_products(place, words, count, tiles, [own, other, below, above, far])

    two = after(two, sums, far_above, far_below)
    far_two = move(two, "z_hi", SWAP)
    late_swapped = [move(p, "core", SWAP) for p in (two, far_above, far_below)]
    sums, soon, n_soon, words, count = tile_products(
        place, words, count, tiles, [*swapped, two], sums, split_rest=True
    )

    far_two = after(far_two, sums)
    last = [far_above, far_below, *late_swapped, far_two, move(far_two, "core", SWAP)]
    z_up, z_two, z_down = tile_products(place, soon, n_soon, tiles, last, sums, owners=(5, 6, 7))
    mine, up_a, up_b, two_a, two_b, down_a, down_b, z_mine = tile_products(
        place, words, count, tiles, last, after(sums, z_two), owners=(0, 1, 2, 3, 4), halved=(1, 2, 3)
    )

    got_two = move(z_two, "z_lo", SWAP)
    got_up = move(z_up, "x", UP)
    got_down = move(z_down, "x", DOWN)
    end_up_b = move(up_b, "x", UP)
    end_down_a = move(down_a, "x", DOWN)
    two_a = move(two_a + got_two[:HALF], "x", UP)
    two_b = move(two_b + got_two[HALF:], "x", DOWN)
    end_z = move(after(z_mine + got_up + got_down, end_up_b, end_down_a), "z_lo", SWAP)
    end_up_a = move(up_a + two_a, "x", UP)
    end_down_b = move(down_b + two_b, "x", DOWN)

    return pl.pallas_call(
        finish_kernel,
        out_shape=jax.ShapeDtypeStruct((BLOCKS * TILE, FEAT), f32),
        compiler_params=pltpu.CompilerParams(vmem_limit_bytes=24 * 2**20),
    )(mine, end_z, end_up_a, end_up_b, end_down_a, end_down_b, weight, bias_vector.reshape(1, FEAT))


def solution(mesh):
    fine = Mesh(mesh.devices.reshape(2, 4, 2, 4, 2), AXES)
    grp, blk = AXES[:2], AXES[2:]
    return jax.shard_map(
        body,
        mesh=fine,
        in_specs=(
            P(AXES, None),
            P(AXES),
            P(grp, blk, None, None, None, None),
            P(grp, blk, None, None),
            P(grp, blk, None, None),
            P(),
            P(),
        ),
        out_specs=P(AXES, None),
        check_vma=False,
    )
```

```python
import functools

import jax
import jax.numpy as jnp
from jax import lax
from jax.experimental import pallas as pl
from jax.experimental.pallas import tpu as pltpu
from jax.sharding import Mesh, PartitionSpec as P

TILE = 128
FEAT = 128
BLOCKS = 8
HALF = 4
SLOTS = 16
BUCKETS = 16
TILES = BUCKETS * SLOTS
STEP = 16
LAST_STEP = 8
RING = 48
DUMMY = 64

AXES = ("z_lo", "x", "z_hi", "y", "core")
UP = [(i, (i + 1) % 4) for i in range(4)]
DOWN = [(i, (i - 1) % 4) for i in range(4)]
SWAP = [(0, 1), (1, 0)]

f32, bf16 = jnp.float32, jnp.bfloat16


def split(v):
    hi = v.astype(bf16)
    return hi, (v - hi.astype(f32)).astype(bf16)


def halves(v):
    return jnp.concatenate(split(v), axis=1)


def product(left, right):
    both = jnp.dot(left, jnp.concatenate([right, right], axis=0), preferred_element_type=f32)
    return both[:, :FEAT] + both[:, FEAT:]


def live_kernel(dest, source, words, count):
    def bucket(k, n):
        loaded = [(dest[k, t], source[k, t]) for t in range(SLOTS)]
        for t, (d, s) in enumerate(loaded):
            words[n] = (k * SLOTS + t) + (k * BLOCKS + s) * 256 + d * 65536
            n = n + (d >= 0).astype(jnp.int32)
        return n

    total = lax.fori_loop(0, BUCKETS, bucket, 0)
    count[0] = total
    for j in range(STEP):
        words[total + j] = -1


def tile_kernel(n_pieces, first, split_rest, owners, *refs):
    place, words, count, tiles = refs[:4]
    refs = refs[4:]
    pieces, refs = refs[:n_pieces], refs[n_pieces:]
    so_far = None if first else refs[0]
    outs = refs[1 - first :]
    if owners:
        parts, (acc, *scratch) = outs[: len(owners)], outs[len(owners) :]
        dummy, size = len(owners) * BLOCKS, LAST_STEP
    else:
        acc, *outs = outs
        rests, (mine, *scratch) = outs[: 2 + 2 * split_rest], outs[2 + 2 * split_rest :]
        dummy, size = DUMMY, STEP
    xs, ring, slots, table, ring_sem, slot_sem = scratch
    depth = RING // size

    with_slots, held, n_blocks = [], [], 0
    for piece in pieces:
        rows = piece.shape[0]
        held.append(n_blocks)
        n_blocks += rows // TILE
        if rows % TILE:
            with_slots.append((piece, n_blocks - BLOCKS))
    reads = [
        pltpu.make_async_copy(piece.at[pl.ds(piece.shape[0] - 8, 8)], slots.at[i], slot_sem.at[i])
        for i, (piece, at) in enumerate(with_slots)
    ]
    for read in reads:
        read.start()

    def fetch(group):
        slot = group % depth
        for j in range(size):
            pltpu.make_async_copy(
                tiles.at[todo[group * size + j] & 255], ring.at[slot, j], ring_sem.at[slot, j]
            ).start()

    def fetch_first():
        for group in range(depth - 1):

            @pl.when(group < groups)
            def _(group=group):
                fetch(group)

    if owners:
        todo, groups = words, (count[0] + size - 1) // size
        fetch_first()

        def begin(j, carry):
            for i, owner in enumerate(owners):
                at = ((owner // 4) ^ place[0]) * 4 + (owner % 4 + place[1] & 3)
                acc[i * BLOCKS + j] = so_far[at * BLOCKS + j]
            return carry

        lax.fori_loop(0, BLOCKS, begin, 0)
    else:
        for p in range(BUCKETS * BLOCKS):
            table[p] = -1

        def begin(d, carry):
            acc[d] = jnp.zeros((TILE, FEAT), f32) if first else so_far[d]
            return carry

        lax.fori_loop(0, DUMMY + 1, begin, 0, unroll=5)
    for read in reads:
        read.wait()
    for i, (piece, at) in enumerate(with_slots):
        for j in range(BLOCKS):
            table[slots[i, 0, j].astype(jnp.int32) & 127] = at + j

    def sort(group, n):
        here, *others = n
        loaded = [words[group * 8 + j] for j in range(8)]
        found = [table[(word >> 8) & 127] for word in loaded]
        for word, s in zip(loaded, found):
            live = (word >= 0).astype(jnp.int32)
            known = jnp.where(s >= 0, live, 0)
            mine[here] = word
            here = here + known
            left = [live - known]
            if split_rest:
                g = word >> 19
                soon = jnp.where((g & 3) != place[1], (g >> 2) ^ place[0], 0) * left[0]
                left = [soon, left[0] - soon]
            for i, more in enumerate(left):
                rests[2 * i][others[i]] = word
                others[i] = others[i] + more
        return (here, *others)

    if not owners:
        here, *others = lax.fori_loop(0, (count[0] + 7) // 8, sort, (0,) * (2 + split_rest))
        for j in range(STEP):
            mine[here + j] = -1
        for i, n in enumerate(others):
            rests[2 * i + 1][0] = n
            for j in range(STEP):
                rests[2 * i][n + j] = -1
        todo, groups = mine, (here + size - 1) // size
        fetch_first()

    def halve(j, carry):
        for piece, at in zip(pieces, held):
            for k in range(0, piece.shape[0] // TILE, HALF):
                rows = pl.ds(pl.multiple_of((k + j) * TILE, TILE), TILE)
                xs[at + k + j] = halves(piece[rows, :])
        return carry

    lax.fori_loop(0, HALF, halve, 0)

    def goal(word):
        if not owners:
            return word >> 16
        g = word >> 19
        distance = ((g >> 2) ^ place[0]) * 4 + ((g & 3) - place[1] & 3)
        return (distance - owners[0]) * BLOCKS + ((word >> 16) & 7)

    def step(group, carry):
        @pl.when(group + depth - 1 < groups)
        def _():
            fetch(group + depth - 1)

        slot = group % depth
        own = [todo[group * size + j] for j in range(size)]
        live = [w >= 0 for w in own]
        source = [jnp.where(l, table[(w >> 8) & 127], 0) for w, l in zip(own, live)]
        target = [jnp.where(l, goal(w), dummy) for w, l in zip(own, live)]
        for j in range(size):
            pltpu.make_async_copy(tiles.at[0], ring.at[slot, j], ring_sem.at[slot, j]).wait()
        results = [product(halves(ring[slot, j]), xs[source[j]]) for j in range(size)]
        for d, result in zip(target, results):
            acc[d] += result
        return carry

    lax.fori_loop(0, groups, step, 0)
    if owners:

        def hand_out(j, carry):
            for i, out in enumerate(parts):
                out[j] = acc[i * BLOCKS + j]
            return carry

        lax.fori_loop(0, BLOCKS, hand_out, 0)


def tile_products(place, words, count, tiles, pieces, so_far=None, split_rest=False, owners=()):
    first = so_far is None
    size = LAST_STEP if owners else STEP
    smem = pl.BlockSpec(memory_space=pltpu.SMEM)
    vmem = pl.BlockSpec(memory_space=pltpu.VMEM)
    hbm = pl.BlockSpec(memory_space=pltpu.HBM)
    listed = [pltpu.SMEM((TILES + 2 * STEP,), jnp.int32), pltpu.SMEM((1,), jnp.int32)]
    rests = listed * (1 + split_rest)
    part = jax.ShapeDtypeStruct((BLOCKS, TILE, FEAT), f32)
    sums = pltpu.VMEM(((len(owners) * BLOCKS or DUMMY) + 1, TILE, FEAT), f32)
    return pl.pallas_call(
        functools.partial(tile_kernel, len(pieces), first, split_rest, owners),
        out_shape=[part] * len(owners)
        or [jax.ShapeDtypeStruct(r.shape, r.dtype) for r in (sums, *rests)],
        in_specs=[smem, smem, smem, hbm] + [vmem] * (len(pieces) + (not first)),
        out_specs=[vmem] * len(owners) or [vmem] + [smem] * len(rests),
        scratch_shapes=[sums if owners else listed[0]]
        + [
            pltpu.VMEM((sum(p.shape[0] // TILE for p in pieces), TILE, 2 * FEAT), bf16),
            pltpu.VMEM((RING // size, size, TILE, TILE), f32),
            pltpu.SMEM((len(pieces), 8, 128), f32),
            pltpu.SMEM((BUCKETS * BLOCKS,), jnp.int32),
            pltpu.SemaphoreType.DMA((RING // size, size)),
            pltpu.SemaphoreType.DMA((len(pieces),)),
        ],
        compiler_params=pltpu.CompilerParams(vmem_limit_bytes=40 * 2**20),
        cost_estimate=pl.CostEstimate(flops=10**5, bytes_accessed=10**4, transcendentals=0),
    )(place, words, count, tiles, *pieces, *([] if first else [so_far]))


def finish_kernel(a, b, c, d, weight, bias, out):
    total = a[...] + b[...] + c[...] + d[...]
    hidden = product(halves(total.reshape(BLOCKS * TILE, FEAT)), halves(weight[...]))
    out[...] = jnp.maximum(hidden + bias[...], 0.0)


def after(value, *others):
    return lax.optimization_barrier((value, *others))[0]


def body(features, new_slot, tile_values, tile_dest, tile_source, weight, bias_vector):
    move = lax.ppermute
    row = jnp.pad(new_slot.astype(f32)[None, :], ((0, 7), (0, FEAT - BLOCKS)))
    own = jnp.concatenate([features, row])
    below = move(own, "y", UP)
    above = move(own, "y", DOWN)
    far = move(own, "z_hi", SWAP)
    other = move(own, "core", SWAP)

    place = jnp.stack([lax.axis_index("z_lo"), lax.axis_index("x")]).astype(jnp.int32)
    tiles = tile_values.reshape(TILES, TILE, TILE)
    smem = pl.BlockSpec(memory_space=pltpu.SMEM)
    words, count = pl.pallas_call(
        live_kernel,
        out_shape=[
            jax.ShapeDtypeStruct((TILES + 2 * STEP,), jnp.int32),
            jax.ShapeDtypeStruct((1,), jnp.int32),
        ],
        in_specs=[smem, smem],
        out_specs=[smem, smem],
        cost_estimate=pl.CostEstimate(flops=10**5, bytes_accessed=10**4, transcendentals=0),
    )(tile_dest.reshape(BUCKETS, SLOTS), tile_source.reshape(BUCKETS, SLOTS))

    below = after(below, words)
    two = move(below, "y", UP)
    far_above = move(far, "y", DOWN)
    far_below = move(below, "z_hi", SWAP)
    swapped = [move(p, "core", SWAP) for p in (above, far)]
    sums, soon, n_soon, words, count = tile_products(
        place, words, count, tiles, [own, other, below, above, far], split_rest=True
    )

    two, far_above, far_below = lax.optimization_barrier((two, far_above, far_below, sums))[:3]
    cut = HALF * TILE
    cuts = [far_below[:cut], far_above[cut:]]
    far_two = [move(cuts[0], "y", UP), move(cuts[1], "y", DOWN)]
    late = [two, far_above, far_below]
    last = [
        *swapped,
        *late,
        *far_two,
        *[move(after(p, *cuts), "core", SWAP) for p in (*late, after(below, sums))],
        *[move(p, "core", SWAP) for p in far_two],
    ]
    z_up, z_two, z_down = tile_products(place, soon, n_soon, tiles, last, sums, owners=(5, 6, 7))
    mine, up, two, down, z_mine = tile_products(
        place, words, count, tiles, last, after(sums, z_two), owners=(0, 1, 2, 3, 4)
    )

    half = BLOCKS // 2
    got_two = move(z_two, "z_lo", SWAP)
    got_up = move(z_up, "x", UP)
    got_down = move(z_down, "x", DOWN)
    two_up = move(two[:half] + got_two[:half], "x", UP)
    two_down = move(two[half:] + got_two[half:], "x", DOWN)
    end_z = move(z_mine + got_up + got_down, "z_lo", SWAP)
    end_up = move(jnp.concatenate([up[:half] + two_up, up[half:]]), "x", UP)
    end_down = move(jnp.concatenate([down[:half], down[half:] + two_down]), "x", DOWN)

    return pl.pallas_call(
        finish_kernel,
        out_shape=jax.ShapeDtypeStruct((BLOCKS * TILE, FEAT), f32),
        compiler_params=pltpu.CompilerParams(vmem_limit_bytes=24 * 2**20),
    )(mine, end_up, end_down, end_z, weight, bias_vector.reshape(1, FEAT))


def solution(mesh):
    fine = Mesh(mesh.devices.reshape(2, 4, 2, 4, 2), AXES)
    grp, blk = AXES[:2], AXES[2:]
    return jax.shard_map(
        body,
        mesh=fine,
        in_specs=(
            P(AXES, None),
            P(AXES),
            P(grp, blk, None, None, None, None),
            P(grp, blk, None, None),
            P(grp, blk, None, None),
            P(),
            P(),
        ),
        out_specs=P(AXES, None),
        check_vma=False,
    )
```

```python
import functools

import jax
import jax.numpy as jnp
from jax import lax
from jax.experimental import pallas as pl
from jax.experimental.pallas import tpu as pltpu
from jax.sharding import Mesh, PartitionSpec as P

TILE = 128
FEAT = 128
BLOCKS = 8
HALF = 4
SLOTS = 16
BUCKETS = 16
TILES = BUCKETS * SLOTS
STEP = 16
LAST_STEP = 8
RING = 48
DUMMY = 64

AXES = ("z_lo", "x", "z_hi", "y", "core")
UP = [(i, (i + 1) % 4) for i in range(4)]
DOWN = [(i, (i - 1) % 4) for i in range(4)]
SWAP = [(0, 1), (1, 0)]

f32, bf16 = jnp.float32, jnp.bfloat16


def split(v):
    hi = v.astype(bf16)
    return hi, (v - hi.astype(f32)).astype(bf16)


def halves(v):
    return jnp.concatenate(split(v), axis=1)


def product(left, right):
    both = jnp.dot(left, jnp.concatenate([right, right], axis=0), preferred_element_type=f32)
    return both[:, :FEAT] + both[:, FEAT:]


def live_kernel(dest, source, words, count):
    def bucket(k, n):
        loaded = [(dest[k, t], source[k, t]) for t in range(SLOTS)]
        for t, (d, s) in enumerate(loaded):
            words[n] = (k * SLOTS + t) + (k * BLOCKS + s) * 256 + d * 65536
            n = n + (d >= 0).astype(jnp.int32)
        return n

    total = lax.fori_loop(0, BUCKETS, bucket, 0)
    count[0] = total
    for j in range(STEP):
        words[total + j] = -1


def cut_up(rows):
    piece = BLOCKS * TILE + 8
    step = piece if rows % piece == 0 else rows
    return [(row, step) for row in range(0, rows, step)]


def tile_kernel(n_pieces, first, split_rest, owners, *refs):
    place, words, count, tiles = refs[:4]
    refs = refs[4:]
    pieces, refs = refs[:n_pieces], refs[n_pieces:]
    so_far = None if first else refs[0]
    outs = refs[1 - first :]
    if owners:
        parts, (acc, *scratch) = outs[: len(owners)], outs[len(owners) :]
        dummy, size = len(owners) * BLOCKS, LAST_STEP
    else:
        acc, *outs = outs
        rests, (mine, *scratch) = outs[: 2 + 2 * split_rest], outs[2 + 2 * split_rest :]
        dummy, size = DUMMY, STEP
    xs, ring, slots, table, ring_sem, slot_sem = scratch
    depth = RING // size

    views, with_slots, n_blocks = [], [], 0
    for piece in pieces:
        for row, rows in cut_up(piece.shape[0]):
            views.append((piece, row, rows // TILE, n_blocks))
            n_blocks += rows // TILE
            if rows % TILE:
                with_slots.append((piece, row + rows - 8, n_blocks - BLOCKS))
    reads = [
        pltpu.make_async_copy(piece.at[pl.ds(row, 8)], slots.at[i], slot_sem.at[i])
        for i, (piece, row, at) in enumerate(with_slots)
    ]
    for read in reads:
        read.start()

    def fetch(group):
        slot = group % depth
        for j in range(size):
            pltpu.make_async_copy(
                tiles.at[todo[group * size + j] & 255], ring.at[slot, j], ring_sem.at[slot, j]
            ).start()

    def fetch_first():
        for group in range(depth - 1):

            @pl.when(group < groups)
            def _(group=group):
                fetch(group)

    if owners:
        todo, groups = words, (count[0] + size - 1) // size
        fetch_first()

        def begin(j, carry):
            for i, owner in enumerate(owners):
                at = ((owner // 4) ^ place[0]) * 4 + (owner % 4 + place[1] & 3)
                acc[i * BLOCKS + j] = so_far[at * BLOCKS + j]
            return carry

        lax.fori_loop(0, BLOCKS, begin, 0)
    else:
        for p in range(BUCKETS * BLOCKS):
            table[p] = -1

        def begin(d, carry):
            acc[d] = jnp.zeros((TILE, FEAT), f32) if first else so_far[d]
            return carry

        lax.fori_loop(0, DUMMY + 1, begin, 0, unroll=5)
    for read in reads:
        read.wait()
    for i, (piece, row, at) in enumerate(with_slots):
        for j in range(BLOCKS):
            table[slots[i, 0, j].astype(jnp.int32) & 127] = at + j

    def sort(group, n):
        here, *others = n
        loaded = [words[group * 8 + j] for j in range(8)]
        found = [table[(word >> 8) & 127] for word in loaded]
        for word, s in zip(loaded, found):
            live = (word >= 0).astype(jnp.int32)
            known = jnp.where(s >= 0, live, 0)
            mine[here] = word
            here = here + known
            left = [live - known]
            if split_rest:
                g = word >> 19
                soon = jnp.where((g & 3) != place[1], (g >> 2) ^ place[0], 0) * left[0]
                left = [soon, left[0] - soon]
            for i, more in enumerate(left):
                rests[2 * i][others[i]] = word
                others[i] = others[i] + more
        return (here, *others)

    if not owners:
        here, *others = lax.fori_loop(0, (count[0] + 7) // 8, sort, (0,) * (2 + split_rest))
        for j in range(STEP):
            mine[here + j] = -1
        for i, n in enumerate(others):
            rests[2 * i + 1][0] = n
            for j in range(STEP):
                rests[2 * i][n + j] = -1
        todo, groups = mine, (here + size - 1) // size
        fetch_first()

    def halve(j, carry):
        for piece, row, blocks, at in views:
            for k in range(0, blocks, HALF):
                rows = pl.ds(pl.multiple_of(row + (k + j) * TILE, 8), TILE)
                xs[at + k + j] = halves(piece[rows, :])
        return carry

    lax.fori_loop(0, HALF, halve, 0)

    def goal(word):
        if not owners:
            return word >> 16
        g = word >> 19
        distance = ((g >> 2) ^ place[0]) * 4 + ((g & 3) - place[1] & 3)
        return (distance - owners[0]) * BLOCKS + ((word >> 16) & 7)

    def step(group, carry):
        @pl.when(group + depth - 1 < groups)
        def _():
            fetch(group + depth - 1)

        slot = group % depth
        own = [todo[group * size + j] for j in range(size)]
        live = [w >= 0 for w in own]
        source = [jnp.where(l, table[(w >> 8) & 127], 0) for w, l in zip(own, live)]
        target = [jnp.where(l, goal(w), dummy) for w, l in zip(own, live)]
        for j in range(size):
            pltpu.make_async_copy(tiles.at[0], ring.at[slot, j], ring_sem.at[slot, j]).wait()
        results = [product(halves(ring[slot, j]), xs[source[j]]) for j in range(size)]
        for d, result in zip(target, results):
            acc[d] += result
        return carry

    lax.fori_loop(0, groups, step, 0)
    if owners:

        def hand_out(j, carry):
            for i, out in enumerate(parts):
                out[j] = acc[i * BLOCKS + j]
            return carry

        lax.fori_loop(0, BLOCKS, hand_out, 0)


def tile_products(place, words, count, tiles, pieces, so_far=None, split_rest=False, owners=()):
    first = so_far is None
    views = [rows for p in pieces for row, rows in cut_up(p.shape[0])]
    n_blocks = sum(rows // TILE for rows in views)
    size = LAST_STEP if owners else STEP
    smem = pl.BlockSpec(memory_space=pltpu.SMEM)
    vmem = pl.BlockSpec(memory_space=pltpu.VMEM)
    hbm = pl.BlockSpec(memory_space=pltpu.HBM)
    listed = [pltpu.SMEM((TILES + 2 * STEP,), jnp.int32), pltpu.SMEM((1,), jnp.int32)]
    rests = listed * (1 + split_rest)
    part = jax.ShapeDtypeStruct((BLOCKS, TILE, FEAT), f32)
    sums = pltpu.VMEM(((len(owners) * BLOCKS or DUMMY) + 1, TILE, FEAT), f32)
    return pl.pallas_call(
        functools.partial(tile_kernel, len(pieces), first, split_rest, owners),
        out_shape=[part] * len(owners)
        or [jax.ShapeDtypeStruct(r.shape, r.dtype) for r in (sums, *rests)],
        in_specs=[smem, smem, smem, hbm] + [vmem] * (len(pieces) + (not first)),
        out_specs=[vmem] * len(owners) or [vmem] + [smem] * len(rests),
        scratch_shapes=[sums if owners else listed[0]]
        + [
            pltpu.VMEM((n_blocks, TILE, 2 * FEAT), bf16),
            pltpu.VMEM((RING // size, size, TILE, TILE), f32),
            pltpu.SMEM((len(views), 8, 128), f32),
            pltpu.SMEM((BUCKETS * BLOCKS,), jnp.int32),
            pltpu.SemaphoreType.DMA((RING // size, size)),
            pltpu.SemaphoreType.DMA((len(views),)),
        ],
        compiler_params=pltpu.CompilerParams(vmem_limit_bytes=38 * 2**20),
        cost_estimate=pl.CostEstimate(flops=10**5, bytes_accessed=10**4, transcendentals=0),
    )(place, words, count, tiles, *pieces, *([] if first else [so_far]))


def finish_kernel(a, b, c, d, weight, bias, out):
    total = a[...] + b[...] + c[...] + d[...]
    hidden = product(halves(total.reshape(BLOCKS * TILE, FEAT)), halves(weight[...]))
    out[...] = jnp.maximum(hidden + bias[...], 0.0)


def after(value, *others):
    return lax.optimization_barrier((value, *others))[0]


def body(features, new_slot, tile_values, tile_dest, tile_source, weight, bias_vector):
    move = lax.ppermute
    row = jnp.pad(new_slot.astype(f32)[None, :], ((0, 7), (0, FEAT - BLOCKS)))
    own = jnp.concatenate([features, row])
    below = move(own, "y", UP)
    above = move(own, "y", DOWN)
    far = move(own, "z_hi", SWAP)
    other = move(own, "core", SWAP)

    place = jnp.stack([lax.axis_index("z_lo"), lax.axis_index("x")]).astype(jnp.int32)
    tiles = tile_values.reshape(TILES, TILE, TILE)
    smem = pl.BlockSpec(memory_space=pltpu.SMEM)
    words, count = pl.pallas_call(
        live_kernel,
        out_shape=[
            jax.ShapeDtypeStruct((TILES + 2 * STEP,), jnp.int32),
            jax.ShapeDtypeStruct((1,), jnp.int32),
        ],
        in_specs=[smem, smem],
        out_specs=[smem, smem],
        cost_estimate=pl.CostEstimate(flops=10**5, bytes_accessed=10**4, transcendentals=0),
    )(tile_dest.reshape(BUCKETS, SLOTS), tile_source.reshape(BUCKETS, SLOTS))

    below = after(below, words)
    two = move(below, "y", UP)
    far_above = move(far, "y", DOWN)
    far_below = move(below, "z_hi", SWAP)
    swapped = move(jnp.concatenate([below, above, far]), "core", SWAP)
    sums, soon, n_soon, words, count = tile_products(
        place, words, count, tiles, [own, other, below, above, far], split_rest=True
    )

    two, far_above, far_below = lax.optimization_barrier((two, far_above, far_below, sums))[:3]
    cut = HALF * TILE
    cuts = [far_below[:cut], far_above[cut:]]
    far_two = [move(cuts[0], "y", UP), move(cuts[1], "y", DOWN)]
    late = [two, far_above, far_below]
    last = [
        swapped,
        *late,
        *far_two,
        move(after(jnp.concatenate(late), *cuts), "core", SWAP),
        *[move(p, "core", SWAP) for p in far_two],
    ]
    z_up, z_two, z_down = tile_products(place, soon, n_soon, tiles, last, sums, owners=(5, 6, 7))
    mine, up, two, down, z_mine = tile_products(
        place, words, count, tiles, last, after(sums, z_two), owners=(0, 1, 2, 3, 4)
    )

    half = BLOCKS // 2
    got_two = move(z_two, "z_lo", SWAP)
    got_up = move(z_up, "x", UP)
    got_down = move(z_down, "x", DOWN)
    two_up = move(two[:half] + got_two[:half], "x", UP)
    two_down = move(two[half:] + got_two[half:], "x", DOWN)
    end_z = move(z_mine + got_up + got_down, "z_lo", SWAP)
    end_up = move(jnp.concatenate([up[:half] + two_up, up[half:]]), "x", UP)
    end_down = move(jnp.concatenate([down[:half], down[half:] + two_down]), "x", DOWN)

    return pl.pallas_call(
        finish_kernel,
        out_shape=jax.ShapeDtypeStruct((BLOCKS * TILE, FEAT), f32),
        compiler_params=pltpu.CompilerParams(vmem_limit_bytes=24 * 2**20),
    )(mine, end_up, end_down, end_z, weight, bias_vector.reshape(1, FEAT))


def solution(mesh):
    fine = Mesh(mesh.devices.reshape(2, 4, 2, 4, 2), AXES)
    grp, blk = AXES[:2], AXES[2:]
    return jax.shard_map(
        body,
        mesh=fine,
        in_specs=(
            P(AXES, None),
            P(AXES),
            P(grp, blk, None, None, None, None),
            P(grp, blk, None, None),
            P(grp, blk, None, None),
            P(),
            P(),
        ),
        out_specs=P(AXES, None),
        check_vma=False,
    )
```

```python
import functools

import jax
import jax.numpy as jnp
from jax import lax
from jax.experimental import pallas as pl
from jax.experimental.pallas import tpu as pltpu
from jax.sharding import Mesh, PartitionSpec as P

TILE = 128
FEAT = 128
BLOCKS = 8
HALF = 4
SLOTS = 16
BUCKETS = 16
TILES = BUCKETS * SLOTS
STEP = 16
LAST_STEP = 8
RING = 48
DUMMY = 64

AXES = ("z_lo", "x", "z_hi", "y", "core")
UP = [(i, (i + 1) % 4) for i in range(4)]
DOWN = [(i, (i - 1) % 4) for i in range(4)]
SWAP = [(0, 1), (1, 0)]

f32, bf16 = jnp.float32, jnp.bfloat16


def split(v):
    hi = v.astype(bf16)
    return hi, (v - hi.astype(f32)).astype(bf16)


def halves(v):
    return jnp.concatenate(split(v), axis=1)


def product(left, right):
    both = jnp.dot(left, jnp.concatenate([right, right], axis=0), preferred_element_type=f32)
    return both[:, :FEAT] + both[:, FEAT:]


def live_kernel(dest, source, words, count):
    def bucket(k, n):
        loaded = [(dest[k, t], source[k, t]) for t in range(SLOTS)]
        for t, (d, s) in enumerate(loaded):
            words[n] = (k * SLOTS + t) + (k * BLOCKS + s) * 256 + d * 65536
            n = n + (d >= 0).astype(jnp.int32)
        return n

    total = lax.fori_loop(0, BUCKETS, bucket, 0)
    count[0] = total
    for j in range(STEP):
        words[total + j] = -1


def cut_up(rows):
    piece = BLOCKS * TILE + 8
    step = piece if rows % piece == 0 else rows
    return [(row, step) for row in range(0, rows, step)]


def tile_kernel(n_pieces, first, split_rest, owners, *refs):
    place, words, count, tiles = refs[:4]
    refs = refs[4:]
    pieces, refs = refs[:n_pieces], refs[n_pieces:]
    so_far = None if first else refs[0]
    outs = refs[1 - first :]
    if owners:
        parts, (acc, *scratch) = outs[: len(owners)], outs[len(owners) :]
        dummy, size = len(owners) * BLOCKS, LAST_STEP
    else:
        acc, *outs = outs
        rests, (mine, *scratch) = outs[: 2 + 2 * split_rest], outs[2 + 2 * split_rest :]
        dummy, size = DUMMY, STEP
    xs, ring, slots, table, ring_sem, slot_sem = scratch
    depth = RING // size

    views, with_slots, n_blocks = [], [], 0
    for piece in pieces:
        for row, rows in cut_up(piece.shape[0]):
            views.append((piece, row, rows // TILE, n_blocks))
            n_blocks += rows // TILE
            if rows % TILE:
                with_slots.append((piece, row + rows - 8, n_blocks - BLOCKS))
    reads = [
        pltpu.make_async_copy(piece.at[pl.ds(row, 8)], slots.at[i], slot_sem.at[i])
        for i, (piece, row, at) in enumerate(with_slots)
    ]
    for read in reads:
        read.start()

    def fetch(group):
        slot = group % depth
        for j in range(size):
            pltpu.make_async_copy(
                tiles.at[todo[group * size + j] & 255], ring.at[slot, j], ring_sem.at[slot, j]
            ).start()

    def fetch_first():
        for group in range(depth - 1):

            @pl.when(group < groups)
            def _(group=group):
                fetch(group)

    if owners:
        todo, groups = words, (count[0] + size - 1) // size
        fetch_first()

        def begin(j, carry):
            for i, owner in enumerate(owners):
                at = ((owner // 4) ^ place[0]) * 4 + (owner % 4 + place[1] & 3)
                acc[i * BLOCKS + j] = so_far[at * BLOCKS + j]
            return carry

        lax.fori_loop(0, BLOCKS, begin, 0)
    else:
        for p in range(BUCKETS * BLOCKS):
            table[p] = -1

        def begin(d, carry):
            acc[d] = jnp.zeros((TILE, FEAT), f32) if first else so_far[d]
            return carry

        lax.fori_loop(0, DUMMY + 1, begin, 0, unroll=5)
    for read in reads:
        read.wait()
    for i, (piece, row, at) in enumerate(with_slots):
        for j in range(BLOCKS):
            table[slots[i, 0, j].astype(jnp.int32) & 127] = at + j

    def sort(group, n):
        here, *others = n
        loaded = [words[group * 8 + j] for j in range(8)]
        found = [table[(word >> 8) & 127] for word in loaded]
        for word, s in zip(loaded, found):
            live = (word >= 0).astype(jnp.int32)
            known = jnp.where(s >= 0, live, 0)
            mine[here] = word
            here = here + known
            left = [live - known]
            if split_rest:
                g = word >> 19
                soon = jnp.where((g & 3) != place[1], (g >> 2) ^ place[0], 0) * left[0]
                left = [soon, left[0] - soon]
            for i, more in enumerate(left):
                rests[2 * i][others[i]] = word
                others[i] = others[i] + more
        return (here, *others)

    if not owners:
        here, *others = lax.fori_loop(0, (count[0] + 7) // 8, sort, (0,) * (2 + split_rest))
        for j in range(STEP):
            mine[here + j] = -1
        for i, n in enumerate(others):
            rests[2 * i + 1][0] = n
            for j in range(STEP):
                rests[2 * i][n + j] = -1
        todo, groups = mine, (here + size - 1) // size
        fetch_first()

    def halve(j, carry):
        for piece, row, blocks, at in views:
            for k in range(0, blocks, HALF):
                rows = pl.ds(pl.multiple_of(row + (k + j) * TILE, 8), TILE)
                xs[at + k + j] = halves(piece[rows, :])
        return carry

    lax.fori_loop(0, HALF, halve, 0)

    def goal(word):
        if not owners:
            return word >> 16
        g = word >> 19
        distance = ((g >> 2) ^ place[0]) * 4 + ((g & 3) - place[1] & 3)
        return (distance - owners[0]) * BLOCKS + ((word >> 16) & 7)

    def step(group, carry):
        @pl.when(group + depth - 1 < groups)
        def _():
            fetch(group + depth - 1)

        slot = group % depth
        own = [todo[group * size + j] for j in range(size)]
        live = [w >= 0 for w in own]
        source = [jnp.where(l, table[(w >> 8) & 127], 0) for w, l in zip(own, live)]
        target = [jnp.where(l, goal(w), dummy) for w, l in zip(own, live)]
        for j in range(size):
            pltpu.make_async_copy(tiles.at[0], ring.at[slot, j], ring_sem.at[slot, j]).wait()
        results = [product(halves(ring[slot, j]), xs[source[j]]) for j in range(size)]
        for d, result in zip(target, results):
            acc[d] += result
        return carry

    lax.fori_loop(0, groups, step, 0)
    if owners:

        def hand_out(j, carry):
            for i, out in enumerate(parts):
                out[j] = acc[i * BLOCKS + j]
            return carry

        lax.fori_loop(0, BLOCKS, hand_out, 0)


def tile_products(place, words, count, tiles, pieces, so_far=None, split_rest=False, owners=()):
    first = so_far is None
    views = [rows for p in pieces for row, rows in cut_up(p.shape[0])]
    n_blocks = sum(rows // TILE for rows in views)
    size = LAST_STEP if owners else STEP
    smem = pl.BlockSpec(memory_space=pltpu.SMEM)
    vmem = pl.BlockSpec(memory_space=pltpu.VMEM)
    hbm = pl.BlockSpec(memory_space=pltpu.HBM)
    listed = [pltpu.SMEM((TILES + 2 * STEP,), jnp.int32), pltpu.SMEM((1,), jnp.int32)]
    rests = listed * (1 + split_rest)
    part = jax.ShapeDtypeStruct((BLOCKS, TILE, FEAT), f32)
    sums = pltpu.VMEM(((len(owners) * BLOCKS or DUMMY) + 1, TILE, FEAT), f32)
    return pl.pallas_call(
        functools.partial(tile_kernel, len(pieces), first, split_rest, owners),
        out_shape=[part] * len(owners)
        or [jax.ShapeDtypeStruct(r.shape, r.dtype) for r in (sums, *rests)],
        in_specs=[smem, smem, smem, hbm] + [vmem] * (len(pieces) + (not first)),
        out_specs=[vmem] * len(owners) or [vmem] + [smem] * len(rests),
        scratch_shapes=[sums if owners else listed[0]]
        + [
            pltpu.VMEM((n_blocks, TILE, 2 * FEAT), bf16),
            pltpu.VMEM((RING // size, size, TILE, TILE), f32),
            pltpu.SMEM((len(views), 8, 128), f32),
            pltpu.SMEM((BUCKETS * BLOCKS,), jnp.int32),
            pltpu.SemaphoreType.DMA((RING // size, size)),
            pltpu.SemaphoreType.DMA((len(views),)),
        ],
        compiler_params=pltpu.CompilerParams(vmem_limit_bytes=38 * 2**20),
        cost_estimate=pl.CostEstimate(flops=10**5, bytes_accessed=10**4, transcendentals=0),
    )(place, words, count, tiles, *pieces, *([] if first else [so_far]))


def finish_kernel(a, b, c, d, weight, bias, out):
    total = a[...] + b[...] + c[...] + d[...]
    hidden = product(halves(total.reshape(BLOCKS * TILE, FEAT)), halves(weight[...]))
    out[...] = jnp.maximum(hidden + bias[...], 0.0)


def after(value, *others):
    return lax.optimization_barrier((value, *others))[0]


def body(features, new_slot, tile_values, tile_dest, tile_source, weight, bias_vector):
    move = lax.ppermute
    row = jnp.pad(new_slot.astype(f32)[None, :], ((0, 7), (0, FEAT - BLOCKS)))
    own = jnp.concatenate([features, row])
    below = move(own, "y", UP)
    above = move(own, "y", DOWN)
    far = move(own, "z_hi", SWAP)
    other = move(own, "core", SWAP)

    place = jnp.stack([lax.axis_index("z_lo"), lax.axis_index("x")]).astype(jnp.int32)
    tiles = tile_values.reshape(TILES, TILE, TILE)
    smem = pl.BlockSpec(memory_space=pltpu.SMEM)
    words, count = pl.pallas_call(
        live_kernel,
        out_shape=[
            jax.ShapeDtypeStruct((TILES + 2 * STEP,), jnp.int32),
            jax.ShapeDtypeStruct((1,), jnp.int32),
        ],
        in_specs=[smem, smem],
        out_specs=[smem, smem],
        cost_estimate=pl.CostEstimate(flops=10**5, bytes_accessed=10**4, transcendentals=0),
    )(tile_dest.reshape(BUCKETS, SLOTS), tile_source.reshape(BUCKETS, SLOTS))

    below = after(below, words)
    two = move(below, "y", UP)
    far_above = move(far, "y", DOWN)
    far_below = move(below, "z_hi", SWAP)
    swapped = move(jnp.concatenate([below, above, far]), "core", SWAP)
    sums, words, count = tile_products(place, words, count, tiles, [own, other, below, above, far])

    two, far_above, far_below = lax.optimization_barrier((two, far_above, far_below, sums))[:3]
    cut = HALF * TILE
    cuts = [far_below[:cut], far_above[cut:]]
    far_two = [move(cuts[0], "y", UP), move(cuts[1], "y", DOWN)]
    late = [two, far_above, far_below]
    sums, soon, n_soon, words, count = tile_products(
        place, words, count, tiles, [swapped, two], sums, split_rest=True
    )
    far_two = list(lax.optimization_barrier((*far_two, sums))[:2])
    last = [
        far_above,
        far_below,
        *far_two,
        move(after(jnp.concatenate(late), *cuts), "core", SWAP),
        *[move(p, "core", SWAP) for p in far_two],
    ]
    z_up, z_two, z_down = tile_products(place, soon, n_soon, tiles, last, sums, owners=(5, 6, 7))
    mine, up, two, down, z_mine = tile_products(
        place, words, count, tiles, last, after(sums, z_two), owners=(0, 1, 2, 3, 4)
    )

    half = BLOCKS // 2
    got_two = move(z_two, "z_lo", SWAP)
    got_up = move(z_up, "x", UP)
    got_down = move(z_down, "x", DOWN)
    two_up = move(two[:half] + got_two[:half], "x", UP)
    two_down = move(two[half:] + got_two[half:], "x", DOWN)
    end_z = move(z_mine + got_up + got_down, "z_lo", SWAP)
    end_up = move(jnp.concatenate([up[:half] + two_up, up[half:]]), "x", UP)
    end_down = move(jnp.concatenate([down[:half], down[half:] + two_down]), "x", DOWN)

    return pl.pallas_call(
        finish_kernel,
        out_shape=jax.ShapeDtypeStruct((BLOCKS * TILE, FEAT), f32),
        compiler_params=pltpu.CompilerParams(vmem_limit_bytes=24 * 2**20),
    )(mine, end_up, end_down, end_z, weight, bias_vector.reshape(1, FEAT))


def solution(mesh):
    fine = Mesh(mesh.devices.reshape(2, 4, 2, 4, 2), AXES)
    grp, blk = AXES[:2], AXES[2:]
    return jax.shard_map(
        body,
        mesh=fine,
        in_specs=(
            P(AXES, None),
            P(AXES),
            P(grp, blk, None, None, None, None),
            P(grp, blk, None, None),
            P(grp, blk, None, None),
            P(),
            P(),
        ),
        out_specs=P(AXES, None),
        check_vma=False,
    )
```

```python
import functools

import jax
import jax.numpy as jnp
from jax import lax
from jax.experimental import pallas as pl
from jax.experimental.pallas import tpu as pltpu
from jax.sharding import Mesh, PartitionSpec as P

TILE = 128
FEAT = 128
BLOCKS = 8
HALF = 4
SLOTS = 16
BUCKETS = 16
TILES = BUCKETS * SLOTS
STEP = 16
LAST_STEP = 8
RING = 48
DUMMY = 64

AXES = ("z_lo", "x", "z_hi", "y", "core")
UP = [(i, (i + 1) % 4) for i in range(4)]
DOWN = [(i, (i - 1) % 4) for i in range(4)]
SWAP = [(0, 1), (1, 0)]

f32, bf16 = jnp.float32, jnp.bfloat16


def split(v):
    hi = v.astype(bf16)
    return hi, (v - hi.astype(f32)).astype(bf16)


def halves(v):
    return jnp.concatenate(split(v), axis=1)


def product(left, right):
    both = jnp.dot(left, jnp.concatenate([right, right], axis=0), preferred_element_type=f32)
    return both[:, :FEAT] + both[:, FEAT:]


def live_kernel(dest, source, words, count):
    def bucket(k, n):
        loaded = [(dest[k, t], source[k, t]) for t in range(SLOTS)]
        for t, (d, s) in enumerate(loaded):
            words[n] = (k * SLOTS + t) + (k * BLOCKS + s) * 256 + d * 65536
            n = n + (d >= 0).astype(jnp.int32)
        return n

    total = lax.fori_loop(0, BUCKETS, bucket, 0)
    count[0] = total
    for j in range(STEP):
        words[total + j] = -1


def cut_up(rows):
    piece = BLOCKS * TILE + 8
    step = piece if rows % piece == 0 else rows
    return [(row, step) for row in range(0, rows, step)]


def tile_kernel(n_pieces, first, split_rest, owners, *refs):
    place, words, count, tiles = refs[:4]
    refs = refs[4:]
    pieces, refs = refs[:n_pieces], refs[n_pieces:]
    so_far = None if first else refs[0]
    outs = refs[1 - first :]
    if owners:
        parts, (acc, *scratch) = outs[: len(owners)], outs[len(owners) :]
        dummy, size = len(owners) * BLOCKS, LAST_STEP
    else:
        acc, *outs = outs
        rests, (mine, *scratch) = outs[: 2 + 2 * split_rest], outs[2 + 2 * split_rest :]
        dummy, size = DUMMY, STEP
    xs, ring, slots, table, ring_sem, slot_sem = scratch
    depth = RING // size

    views, with_slots, n_blocks = [], [], 0
    for piece in pieces:
        for row, rows in cut_up(piece.shape[0]):
            views.append((piece, row, rows // TILE, n_blocks))
            n_blocks += rows // TILE
            if rows % TILE:
                with_slots.append((piece, row + rows - 8, n_blocks - BLOCKS))
    reads = [
        pltpu.make_async_copy(piece.at[pl.ds(row, 8)], slots.at[i], slot_sem.at[i])
        for i, (piece, row, at) in enumerate(with_slots)
    ]
    for read in reads:
        read.start()

    def fetch(group):
        slot = group % depth
        for j in range(size):
            pltpu.make_async_copy(
                tiles.at[todo[group * size + j] & 255], ring.at[slot, j], ring_sem.at[slot, j]
            ).start()

    def fetch_first():
        for group in range(depth - 1):

            @pl.when(group < groups)
            def _(group=group):
                fetch(group)

    if owners:
        todo, groups = words, (count[0] + size - 1) // size
        fetch_first()

        def begin(j, carry):
            for i, owner in enumerate(owners):
                at = ((owner // 4) ^ place[0]) * 4 + (owner % 4 + place[1] & 3)
                acc[i * BLOCKS + j] = so_far[at * BLOCKS + j]
            return carry

        lax.fori_loop(0, BLOCKS, begin, 0)
    else:
        for p in range(BUCKETS * BLOCKS):
            table[p] = -1

        def begin(d, carry):
            acc[d] = jnp.zeros((TILE, FEAT), f32) if first else so_far[d]
            return carry

        lax.fori_loop(0, DUMMY + 1, begin, 0, unroll=5)
    for read in reads:
        read.wait()
    for i, (piece, row, at) in enumerate(with_slots):
        for j in range(BLOCKS):
            table[slots[i, 0, j].astype(jnp.int32) & 127] = at + j

    def sort(group, n):
        here, *others = n
        loaded = [words[group * 8 + j] for j in range(8)]
        found = [table[(word >> 8) & 127] for word in loaded]
        for word, s in zip(loaded, found):
            live = (word >= 0).astype(jnp.int32)
            known = jnp.where(s >= 0, live, 0)
            mine[here] = word
            here = here + known
            left = [live - known]
            if split_rest:
                g = word >> 19
                soon = jnp.where((g & 3) != place[1], (g >> 2) ^ place[0], 0) * left[0]
                left = [soon, left[0] - soon]
            for i, more in enumerate(left):
                rests[2 * i][others[i]] = word
                others[i] = others[i] + more
        return (here, *others)

    if not owners:
        here, *others = lax.fori_loop(0, (count[0] + 7) // 8, sort, (0,) * (2 + split_rest))
        for j in range(STEP):
            mine[here + j] = -1
        for i, n in enumerate(others):
            rests[2 * i + 1][0] = n
            for j in range(STEP):
                rests[2 * i][n + j] = -1
        todo, groups = mine, (here + size - 1) // size
        fetch_first()

    def halve(j, carry):
        for piece, row, blocks, at in views:
            for k in range(0, blocks, HALF):
                rows = pl.ds(pl.multiple_of(row + (k + j) * TILE, 8), TILE)
                xs[at + k + j] = halves(piece[rows, :])
        return carry

    lax.fori_loop(0, HALF, halve, 0)

    def goal(word):
        if not owners:
            return word >> 16
        g = word >> 19
        distance = ((g >> 2) ^ place[0]) * 4 + ((g & 3) - place[1] & 3)
        return (distance - owners[0]) * BLOCKS + ((word >> 16) & 7)

    def step(group, carry):
        @pl.when(group + depth - 1 < groups)
        def _():
            fetch(group + depth - 1)

        slot = group % depth
        own = [todo[group * size + j] for j in range(size)]
        live = [w >= 0 for w in own]
        source = [jnp.where(l, table[(w >> 8) & 127], 0) for w, l in zip(own, live)]
        target = [jnp.where(l, goal(w), dummy) for w, l in zip(own, live)]
        for j in range(size):
            pltpu.make_async_copy(tiles.at[0], ring.at[slot, j], ring_sem.at[slot, j]).wait()
        results = [product(halves(ring[slot, j]), xs[source[j]]) for j in range(size)]
        for d, result in zip(target, results):
            acc[d] += result
        return carry

    lax.fori_loop(0, groups, step, 0)
    if owners:

        def hand_out(j, carry):
            for i, out in enumerate(parts):
                out[j] = acc[i * BLOCKS + j]
            return carry

        lax.fori_loop(0, BLOCKS, hand_out, 0)


def tile_products(place, words, count, tiles, pieces, so_far=None, split_rest=False, owners=()):
    first = so_far is None
    views = [rows for p in pieces for row, rows in cut_up(p.shape[0])]
    n_blocks = sum(rows // TILE for rows in views)
    size = LAST_STEP if owners else STEP
    smem = pl.BlockSpec(memory_space=pltpu.SMEM)
    vmem = pl.BlockSpec(memory_space=pltpu.VMEM)
    hbm = pl.BlockSpec(memory_space=pltpu.HBM)
    listed = [pltpu.SMEM((TILES + 2 * STEP,), jnp.int32), pltpu.SMEM((1,), jnp.int32)]
    rests = listed * (1 + split_rest)
    part = jax.ShapeDtypeStruct((BLOCKS, TILE, FEAT), f32)
    sums = pltpu.VMEM(((len(owners) * BLOCKS or DUMMY) + 1, TILE, FEAT), f32)
    return pl.pallas_call(
        functools.partial(tile_kernel, len(pieces), first, split_rest, owners),
        out_shape=[part] * len(owners)
        or [jax.ShapeDtypeStruct(r.shape, r.dtype) for r in (sums, *rests)],
        in_specs=[smem, smem, smem, hbm] + [vmem] * (len(pieces) + (not first)),
        out_specs=[vmem] * len(owners) or [vmem] + [smem] * len(rests),
        scratch_shapes=[sums if owners else listed[0]]
        + [
            pltpu.VMEM((n_blocks, TILE, 2 * FEAT), bf16),
            pltpu.VMEM((RING // size, size, TILE, TILE), f32),
            pltpu.SMEM((len(views), 8, 128), f32),
            pltpu.SMEM((BUCKETS * BLOCKS,), jnp.int32),
            pltpu.SemaphoreType.DMA((RING // size, size)),
            pltpu.SemaphoreType.DMA((len(views),)),
        ],
        compiler_params=pltpu.CompilerParams(vmem_limit_bytes=38 * 2**20),
        cost_estimate=pl.CostEstimate(flops=10**5, bytes_accessed=10**4, transcendentals=0),
    )(place, words, count, tiles, *pieces, *([] if first else [so_far]))


def finish_kernel(a, b, c, d, weight, bias, out):
    total = a[...] + b[...] + c[...] + d[...]
    hidden = product(halves(total.reshape(BLOCKS * TILE, FEAT)), halves(weight[...]))
    out[...] = jnp.maximum(hidden + bias[...], 0.0)


def after(value, *others):
    return lax.optimization_barrier((value, *others))[0]


def body(features, new_slot, tile_values, tile_dest, tile_source, weight, bias_vector):
    move = lax.ppermute
    row = jnp.pad(new_slot.astype(f32)[None, :], ((0, 7), (0, FEAT - BLOCKS)))
    own = jnp.concatenate([features, row])
    below = move(own, "y", UP)
    above = move(own, "y", DOWN)
    far = move(own, "z_hi", SWAP)
    other = move(own, "core", SWAP)

    place = jnp.stack([lax.axis_index("z_lo"), lax.axis_index("x")]).astype(jnp.int32)
    tiles = tile_values.reshape(TILES, TILE, TILE)
    smem = pl.BlockSpec(memory_space=pltpu.SMEM)
    words, count = pl.pallas_call(
        live_kernel,
        out_shape=[
            jax.ShapeDtypeStruct((TILES + 2 * STEP,), jnp.int32),
            jax.ShapeDtypeStruct((1,), jnp.int32),
        ],
        in_specs=[smem, smem],
        out_specs=[smem, smem],
        cost_estimate=pl.CostEstimate(flops=10**5, bytes_accessed=10**4, transcendentals=0),
    )(tile_dest.reshape(BUCKETS, SLOTS), tile_source.reshape(BUCKETS, SLOTS))

    below = after(below, words)
    two = move(below, "y", UP)
    far_above = move(far, "y", DOWN)
    far_below = move(below, "z_hi", SWAP)
    swapped = move(jnp.concatenate([below, above, far]), "core", SWAP)
    sums, words, count = tile_products(place, words, count, tiles, [own, other, below, above, far])

    two, far_above, far_below = lax.optimization_barrier((two, far_above, far_below, sums))[:3]
    cut = HALF * TILE
    cuts = [far_below[:cut], far_above[cut:]]
    far_two = [move(cuts[0], "y", UP), move(cuts[1], "y", DOWN)]
    late = [two, far_above, far_below]
    sums, soon, n_soon, words, count = tile_products(
        place, words, count, tiles, [swapped, two], sums, split_rest=True
    )
    far_two = list(lax.optimization_barrier((*far_two, sums))[:2])
    last = [
        far_above,
        far_below,
        *far_two,
        move(after(jnp.concatenate(late), *cuts), "core", SWAP),
        *[move(p, "core", SWAP) for p in far_two],
    ]
    z_up, z_two, z_down = tile_products(place, soon, n_soon, tiles, last, sums, owners=(5, 6, 7))
    mine, up, two, down, z_mine = tile_products(
        place, words, count, tiles, last, after(sums, z_two), owners=(0, 1, 2, 3, 4)
    )

    half = BLOCKS // 2
    got_two = move(z_two, "z_lo", SWAP)
    got_up = move(z_up, "x", UP)
    got_down = move(z_down, "x", DOWN)
    two_up = move(two[:half] + got_two[:half], "x", UP)
    two_down = move(two[half:] + got_two[half:], "x", DOWN)
    end_z = move(after(z_mine + got_up + got_down, two_up), "z_lo", SWAP)
    end_up = move(jnp.concatenate([up[:half] + two_up, up[half:]]), "x", UP)
    end_down = move(jnp.concatenate([down[:half], down[half:] + two_down]), "x", DOWN)

    return pl.pallas_call(
        finish_kernel,
        out_shape=jax.ShapeDtypeStruct((BLOCKS * TILE, FEAT), f32),
        compiler_params=pltpu.CompilerParams(vmem_limit_bytes=24 * 2**20),
    )(mine, end_up, end_down, end_z, weight, bias_vector.reshape(1, FEAT))


def solution(mesh):
    fine = Mesh(mesh.devices.reshape(2, 4, 2, 4, 2), AXES)
    grp, blk = AXES[:2], AXES[2:]
    return jax.shard_map(
        body,
        mesh=fine,
        in_specs=(
            P(AXES, None),
            P(AXES),
            P(grp, blk, None, None, None, None),
            P(grp, blk, None, None),
            P(grp, blk, None, None),
            P(),
            P(),
        ),
        out_specs=P(AXES, None),
        check_vma=False,
    )
```
